128 devices in a mesh: gx: 8 (over x, core), gy: 16 (over y, z).
Axes of the slice: x: 4, y: 4, z: 4, core: 2. Of those that a mesh axis runs over, the one named last changes fastest.
Arguments:
- gcm_state: float32 [64, 256, 144], P('gx', 'gy'), may hold values from -6 to 6
- crm_state: bfloat16 [128, 128, 2, 2, 3712], P(('gx', 'gy')), may hold values from -6 to 6
- owners: int32 [128, 128, 1], P(('gx', 'gy')), may hold values from 0 to 127; in each aligned block of 128 rows (0 to 127, 128 to 255, ..., all dimensions but the last counted through in order) at most 2 rows name the same one
- ice_mask: int32 [64, 256, 58], P('gx', 'gy'), may hold values 0 or 1
- horizontal_operator: bfloat16 [2, 64, 64], replicated, may hold values from -1 to 2
- vertical_inverse: bfloat16 [2, 58, 58], replicated, may hold values from -1 to 2
- diffusivity: float32 [144], replicated, may hold values from 0.02 to 0.2
Outputs:
- gcm_out: float32 [64, 256, 144], P('gx', 'gy')
- crm_out: bfloat16 [128, 128, 2, 2, 3712], P(('gx', 'gy'))
The draws below stay inside these ranges and needn't reach their ends.
Inputs may be any that keep to these rules, and one draw needn't show every extreme that they name: `owners`: among one device's columns at most 2 name the same owner, a bound that some block reaches.
All inputs are finite; a program needn't handle non-finite values. No bound on the sum of `ice_mask` on one device may be relied on, other than what follows from the above.
Results may differ from the reference program's by a relative error of at most 0.0055.
Values may be sent and summed in bfloat16 or wider, within the bound.
A program may use at most 64 MiB of HBM per device.

```python
import math
import jax
import jax.numpy as jnp
import numpy as np
from jax import lax

LEV = 72
CLEV = 58
CX = 64
VARS = 2
SUBSTEPS = 4
EX = 8
EY = 16
OWNERS = 128
COL_DEV = 128
CAP = 2
NXG = 64
NYG = 256
WIDTH = 144
CROSS = 3712
N_GX = 8
N_GY = 16


def operator_draw(key, order, diagonal, spread):
    noise = jax.random.uniform(key, (VARS, order, order), jnp.float32, -1.0, 1.0)
    return (diagonal * jnp.eye(order, dtype=jnp.float32)[None] + spread / math.sqrt(order) * noise).astype(jnp.bfloat16)


def draw_horizontal_operator(key, part):
    key = jax.random.fold_in(key, 11)
    return operator_draw(key, CX, 0.6, 0.7)


def draw_vertical_inverse(key, part):
    key = jax.random.fold_in(key, 23)
    return operator_draw(key, CLEV, 0.6, 0.7)


def with_ends(result, rng, smallest, largest):
    extent = result.shape
    spot = [jax.random.randint(jax.random.fold_in(rng, axis), (), 0, extent[axis]) for axis in range(len(extent))]
    result = result.at[tuple(spot)].set(smallest)
    longest = extent.index(max(extent))
    spot[longest] = (spot[longest] + 1) % extent[longest]
    return result.at[tuple(spot)].set(largest)


def steps_of(stream_key, extent, shards, low, largest):
    loudness, own = 1.0, jax.random.fold_in(stream_key, 6)
    for dim, parts in shards:
        draws = jnp.exp(jax.random.uniform(jax.random.fold_in(own, dim), (parts,), jnp.float32, low / len(shards), largest / len(shards)))
        loudness = loudness * jnp.repeat(draws, extent[dim] // parts).reshape([-1 if axis == dim else 1 for axis in range(len(extent))])
    return loudness


def shared_out(stream_key, own, number, rows, count, top, most, lean):
    order = jax.random.permutation(stream_key, count)
    packed, usual = load_shares(count, rows * top, most, lean, True), load_shares(count, rows * top, most, lean, False)
    places = jnp.arange(count)

    def named(sizes, turn):
        used = int((sizes > 0).sum())
        fixed = max(1, used // 4)
        moved = fixed + (places - fixed + turn * (used - fixed)) % max(1, count - fixed)
        return jnp.zeros((count,), jnp.int32).at[order[jnp.where(places < fixed, places, moved)]].set(jnp.asarray(sizes, jnp.int32))

    sizes = jnp.where(number % 4 == 0, named(packed, number // 4), named(usual, number - number // 4 - 1))
    mixed = jax.random.permutation(jax.random.fold_in(own, 3), count)
    giver, receiver = mixed[0:count // 2 * 2:2], mixed[1:count // 2 * 2:2]
    margin = jnp.minimum(sizes[giver] - 1, most - sizes[receiver]) // 2
    margin = jnp.where((giver == order[0]) | (receiver == order[0]) | (sizes[receiver] == 0), 0, jnp.maximum(margin, 0))
    moved = jax.random.randint(jax.random.fold_in(own, 4), (count // 2,), 0, 1 << 20) % (margin + 1)
    sizes = sizes.at[giver].add(-moved).at[receiver].add(moved)
    members = jnp.searchsorted(jnp.cumsum(sizes), jnp.arange(rows * top), side="right").astype(jnp.int32)
    listing = members.reshape(top, rows).T
    listing = listing[jax.random.permutation(jax.random.fold_in(own, 1), rows)]
    turn = jax.random.randint(jax.random.fold_in(own, 2), (rows, 1), 0, top)
    return jnp.take_along_axis(listing, (jnp.arange(top)[None, :] + turn) % top, axis=1)


def load_shares(amount, total, limit, lean, full):
    weights = [(1 << 20) // math.isqrt(rank ** lean) + 1 for rank in range(1, amount + 1)]
    largest = limit if full else min(limit, max(-(-total // amount), total * weights[0] // sum(weights)))
    least = 1 if total - largest >= amount - 1 else 0
    counts, surplus = [largest] + [least] * (amount - 1), total - largest - least * (amount - 1)
    while surplus > 0:
        candidates = [i for i in range(1, amount) if counts[i] < largest] or [i for i in range(1, amount) if counts[i] < limit]
        mass, remaining = sum([weights[i] for i in candidates]), surplus
        for i in candidates:
            extra = min(limit - counts[i], max(1, remaining * weights[i] // mass), surplus)
            counts[i] = counts[i] + extra
            surplus = surplus - extra
    return np.array(counts)


def scatter_about(own_key, extent, width, limit, split=(), held_as=jnp.bfloat16):
    array = width * jax.random.normal(own_key, extent, jnp.float32)
    if split:
        array = array * steps_of(own_key, extent, split, -0.22, 0.18)
    return jnp.clip(array, -limit, limit).astype(held_as)


def setup_inputs(seed: int = 0) -> dict:
    seeds = jax.random.split(jax.random.key(seed), 8)
    gcm_state = scatter_about(seeds[0], (NXG, NYG, WIDTH), 1.0, 6.0, ((0, 8), (1, 16)), jnp.float32)
    crm_state = scatter_about(seeds[1], (OWNERS, OWNERS, CAP, VARS, CROSS), 1.0, 6.0, ((0, 128),))
    owners_keys = jax.random.split(jax.random.fold_in(seeds[2], 1), OWNERS * COL_DEV // COL_DEV)
    owners_turns = jax.random.permutation(jax.random.fold_in(seeds[2], 3), OWNERS * COL_DEV // COL_DEV)
    owners = jax.vmap(lambda own, number: shared_out(jax.random.fold_in(seeds[2], 2), own, number, COL_DEV, OWNERS, 1, CAP, 2))(owners_keys, owners_turns).reshape((OWNERS, COL_DEV, 1))
    ice_mask = with_ends((jax.random.randint(seeds[3], (NXG, NYG, CLEV), 0, 2) < 1).astype(jnp.int32), jax.random.fold_in(seeds[3], 1), 0, 1)
    horizontal_operator = draw_horizontal_operator(jax.random.fold_in(seeds[7], 71), 0)
    vertical_inverse = draw_vertical_inverse(jax.random.fold_in(seeds[7], 71), 0)
    diffusivity = jnp.clip(jnp.exp(jax.random.uniform(seeds[6], (WIDTH,), jnp.float32, math.log(0.02), math.log(0.2))), 0.02, 0.2)
    return {"gcm_state": gcm_state, "crm_state": crm_state, "owners": owners, "ice_mask": ice_mask, "horizontal_operator": horizontal_operator, "vertical_inverse": vertical_inverse, "diffusivity": diffusivity}


relax_rate = 0.25
water_share = 0.5
latent_heat = 0.5
ice_rate = 0.2
liquid_rate = 0.4


def level_map(rows, cols):
    place = jnp.arange(rows, dtype=jnp.float32) * ((cols - 1) / (rows - 1))
    table = jnp.maximum(0.0, 1.0 - jnp.abs(place[:, None] - jnp.arange(cols, dtype=jnp.float32)[None, :]))
    return table.astype(jnp.bfloat16)


def cloud_model(state, drive, horizontal_operator, vertical_inverse):
    profile = drive[:, :VARS].astype(jnp.float32)
    ice_rows = drive[:, VARS].astype(jnp.float32)[:, :, None]
    current = state
    hop = horizontal_operator.astype(jnp.float32)
    vinv = vertical_inverse.astype(jnp.float32)
    for substep in range(SUBSTEPS):
        wide = current.astype(jnp.float32)
        spread = jnp.einsum("nvzx,vxy->nvzy", wide, hop)
        column_mean = jnp.mean(wide, axis=3)
        forced = spread + relax_rate * (profile - column_mean)[..., None]
        energy = forced[:, 0]
        water = forced[:, 1]
        excess = water - water_share * energy
        condensed = ice_rows * ice_rate * excess + (1.0 - ice_rows) * liquid_rate * jax.nn.softplus(excess)
        mixed = jnp.stack([energy + latent_heat * condensed, water - condensed], axis=1).astype(jnp.bfloat16)
        current = jnp.einsum("vzk,nvkx->nvzx", vinv, mixed.astype(jnp.float32)).astype(jnp.bfloat16)
    tendency = jnp.mean(current.astype(jnp.float32) - state.astype(jnp.float32), axis=3).astype(jnp.bfloat16)
    return current, tendency


def reference(gcm_state, crm_state, owners, ice_mask, horizontal_operator, vertical_inverse, diffusivity):
    gcm_cols = gcm_state.reshape(N_GX, EX, N_GY, EY, WIDTH).transpose(0, 2, 1, 3, 4).reshape(OWNERS, COL_DEV, VARS, LEV)
    mask_cols = ice_mask.reshape(N_GX, EX, N_GY, EY, CLEV).transpose(0, 2, 1, 3, 4).reshape(OWNERS, COL_DEV, CLEV)
    targets = owners[:, :, 0]
    onehot = (targets[:, :, None] == jnp.arange(OWNERS, dtype=jnp.int32)[None, None, :]).astype(jnp.int32)
    slot_rank = jnp.sum(jnp.cumsum(onehot, axis=1) * onehot, axis=2) - 1
    state_low = gcm_cols.astype(jnp.bfloat16).astype(jnp.float32)
    map_down = level_map(CLEV, LEV).astype(jnp.float32)
    profiles = jnp.einsum("dcvl,zl->dcvz", state_low, map_down, precision=lax.Precision.HIGHEST)
    flags = mask_cols[:, :, None, :].astype(jnp.float32)
    drive = jnp.concatenate([profiles, flags, jnp.ones_like(flags)], axis=2).astype(jnp.bfloat16)
    source = jnp.broadcast_to(jnp.arange(OWNERS, dtype=jnp.int32)[:, None], targets.shape)
    state_cols = crm_state[targets, source, slot_rank].reshape(OWNERS, COL_DEV, VARS, CLEV, CX)

    def per_device(item):
        return cloud_model(item[0], item[1], horizontal_operator, vertical_inverse)

    evolved, tendency = lax.map(per_device, (state_cols, drive))
    crm_out = crm_state.at[targets, source, slot_rank].set(evolved.reshape(OWNERS, COL_DEV, VARS, CROSS))
    map_up = level_map(LEV, CLEV).astype(jnp.float32)
    gained = jnp.einsum("dcvz,lz->dcvl", tendency.astype(jnp.float32), map_up, precision=lax.Precision.HIGHEST)
    updated = gcm_cols + gained
    updated = updated.reshape(N_GX, N_GY, EX, EY, WIDTH).transpose(0, 2, 1, 3, 4).reshape(NXG, NYG, WIDTH)
    neighbours = jnp.roll(updated, 1, 0) + jnp.roll(updated, -1, 0) + jnp.roll(updated, 1, 1) + jnp.roll(updated, -1, 1)
    gcm_out = updated + diffusivity * (neighbours - 4.0 * updated)
    return gcm_out, crm_out
```

```python
import jax
import jax.numpy as jnp
import numpy as np
from jax import lax
from jax.experimental import pallas as pl
from jax.experimental.pallas import tpu as pltpu
from jax.sharding import PartitionSpec as P

BF, F32 = jnp.bfloat16, jnp.float32
SUBSTEPS, CLEV, CX, LEV, COLS = 4, 58, 64, 72, 128
BLOCKS, ROWS = 32, 464


def level_map(rows, cols):
    place = np.arange(rows, dtype=np.float32) * np.float32((cols - 1) / (rows - 1))
    table = np.maximum(0.0, 1.0 - np.abs(place[:, None] - np.arange(cols, dtype=np.float32)[None, :]))
    return table.astype(jnp.bfloat16).astype(np.float32)


def spot(level):
    return (level % 2) * 32 + level // 2


def tables():
    down, up = level_map(CLEV, LEV), level_map(LEV, CLEV)
    at = np.array([spot(l) for l in range(CLEV)])
    drive = np.zeros((2, 144, 384), np.float32)
    flag = np.zeros((2, CLEV, 384), np.float32)
    one = np.zeros((2, 1, 384), np.float32)
    lift = np.zeros((256, 144), np.float32)
    for j in range(2):
        for v in range(2):
            for l in range(CLEV):
                drive[j, v * LEV : (v + 1) * LEV, (v * 2 + j) * 64 + at[l]] = down[l]
                lift[(v * 2 + j) * 64 + at[l], v * LEV : (v + 1) * LEV] = up[:, l]
        flag[j, np.arange(CLEV), 256 + j * 64 + at] = 1.0
        one[j, 0, 256 + j * 64 : 256 + (j + 1) * 64] = 2.0
    rows = np.zeros((256, CLEV), np.float32)
    for g in range(4):
        rows[g * 64 + at, np.arange(CLEV)] = 1.0
    tile = np.tile(np.eye(CX, dtype=np.float32), (4, 1))
    k = np.arange(256)
    first = np.zeros((256, 256), np.float32)
    i2, p, c = k // 128, k // 64 % 2, k % 64
    for a in range(256):
        first[a, p[a] * 128 + i2[a] * 64 + c[a]] = 1.0
    ind = np.zeros((8, 256), np.float32)
    for i in range(4):
        ind[i, i * 64 : (i + 1) * 64] = 1.0
    bf = lambda t: jnp.asarray(t.astype(jnp.bfloat16))
    return dict(
        drive=bf(drive), flag=bf(flag), one=jnp.asarray(one), lift=bf(lift), rows=bf(rows), tile=bf(tile),
        first=bf(first), back=bf(first.T), ind=bf(ind),
    )


def dot(a, b, ca=1, cb=0):
    return lax.dot_general(a, b, (((ca,), (cb,)), ((), ())), preferred_element_type=F32)


def onehots(owners_row):
    o = lax.broadcasted_iota(jnp.int32, (COLS, COLS), 0)
    c = lax.broadcasted_iota(jnp.int32, (COLS, COLS), 1)
    same = jnp.where(owners_row == o, 1.0, 0.0)
    rank = dot(same.astype(BF), jnp.where(o < c, 1.0, 0.0).astype(BF))
    first = jnp.where(rank < 0.5, same, 0.0)
    return first.astype(BF), (same - first).astype(BF)


def outgoing(gcm, ice, m0, m1, drive, flag, one):
    low = gcm.astype(BF)
    ice = ice.astype(F32).astype(BF)
    total = 0.0
    for j, m in enumerate((m0, m1)):
        d = (dot(low, drive[j]) + dot(ice, flag[j]) + one[j]).astype(BF)
        total = total + dot(m, d)
    return total


def operators(h_ref, v_ref, tile, rows, first, hf_s, hb_s, vb_s):
    a = lax.broadcasted_iota(jnp.int32, (256, 256), 0) // 64
    b = lax.broadcasted_iota(jnp.int32, (256, 256), 1) // 64
    diag = a == b
    for v in range(2):
        h = (h_ref[v].astype(F32) - 1.0 / 256.0).astype(BF)
        wide = dot(dot(tile, h).astype(BF), tile, 1, 1)
        hb = jnp.where(diag, wide, 0.0).astype(BF)
        hb_s[v] = hb
        hf_s[v] = dot(hb, first).astype(BF)
    v0 = dot(dot(rows, v_ref[0]).astype(BF), rows, 1, 1)
    v1 = dot(dot(rows, v_ref[1]).astype(BF), rows, 1, 1)
    vb_s[...] = jnp.where(diag, jnp.where(a < 2, v0, v1), 0.0).astype(BF)


def to_work(halves):
    return jnp.concatenate(
        [
            jnp.concatenate([half[j * 32 : (j + 1) * 32, p * 128 : (p + 1) * 128] for half in halves], axis=1)
            for j in range(2)
            for p in range(2)
        ],
        axis=0,
    )


def block(b, x_ref, arr_ref, out_ref, tend_ref, hf_s, hb_s, vb_s, first, back, ind, sx):
    at = pl.ds(pl.multiple_of(b * ROWS, 16), ROWS)
    sx[pl.ds(0, ROWS), :] = x_ref[at, :].astype(F32)
    part = {}
    for v in range(2):
        for h in range(2):
            part[v, h] = jnp.concatenate(
                [
                    jnp.concatenate(
                        [sx[pl.ds(58 * ((2 * h + i) * 2 + j) + v, 32, stride=2), :] for i in range(2)], axis=1
                    )
                    for j in range(2)
                ],
                axis=0,
            ).astype(BF)
    arr = arr_ref[pl.ds(4 * b, 4), 0, :].astype(BF)
    spread = ind[0:4, :]
    force = dot(arr[:, 0:256], spread, 0, 0) * 0.25
    flags = dot(arr[:, 256:384], spread, 0, 0)
    ice = flags > 2.5
    taken = flags > 1.0
    start = [to_work([dot(part[v, h], first) for h in range(2)]) for v in range(2)]
    state = None
    for step in range(SUBSTEPS):
        if step == 0:
            f = [to_work([dot(part[v, h], hf_s[v]) for h in range(2)]) for v in range(2)]
        else:
            f = [dot(state[v * 128 : (v + 1) * 128], hb_s[v]) for v in range(2)]
        f0 = f[0] + force[0:128]
        f1 = f[1] + force[128:256]
        e = f1 - 0.5 * f0
        soft = jnp.maximum(e, 0.0) + jnp.log(1.0 + jnp.exp(-jnp.abs(e)))
        q = jnp.where(ice, 0.2 * e, 0.4 * soft)
        y = jnp.concatenate([(f0 + 0.5 * q).astype(BF), (f1 - q).astype(BF)], axis=0)
        new = dot(vb_s[...], y)
        state = new.astype(BF)
    old = jnp.concatenate(start, axis=0)
    final = state.astype(F32)
    tend = dot(ind, (final - old).astype(BF), 1, 1) * (1.0 / 64.0)
    tend_ref[pl.ds(4 * b, 4), 0, :] = tend[0:4].astype(BF).astype(F32)
    both = jnp.concatenate([taken, taken], axis=0)
    final = jnp.where(both, final, old).astype(BF)
    for v in range(2):
        for h in range(2):
            wide = jnp.concatenate(
                [
                    jnp.concatenate(
                        [
                            final[((v * 2 + j) * 2 + p) * 32 : ((v * 2 + j) * 2 + p + 1) * 32, h * 128 : (h + 1) * 128]
                            for p in range(2)
                        ],
                        axis=1,
                    )
                    for j in range(2)
                ],
                axis=0,
            )
            res = dot(wide, back)
            for j in range(2):
                for i in range(2):
                    sx[pl.ds(58 * ((2 * h + i) * 2 + j) + v, 29, stride=2), :] = res[
                        j * 32 : j * 32 + 29, i * 128 : (i + 1) * 128
                    ]
    out_ref[at, :] = sx[pl.ds(0, ROWS), :].astype(BF)


def send_kernel(gcm_ref, own_ref, ice_ref, drive_ref, flag_ref, one_ref, out_ref):
    m0, m1 = onehots(own_ref[...])
    out_ref[:, 0, :] = outgoing(gcm_ref[...], ice_ref[...], m0, m1, drive_ref, flag_ref, one_ref)


def cloud_kernel(
    x_ref, arr_ref, h_ref, v_ref, tile_ref, rows_ref, first_ref, back_ref, ind_ref,
    out_ref, tend_ref, hf_s, hb_s, vb_s, sx,
):
    operators(h_ref, v_ref, tile_ref[...], rows_ref[...], first_ref[...], hf_s, hb_s, vb_s)
    sx[:, pl.ds(ROWS, 8), :] = jnp.zeros((2, 8, 128), F32)

    def body(t, carry):
        for k in range(2):
            block(
                2 * t + k, x_ref, arr_ref, out_ref, tend_ref, hf_s, hb_s, vb_s,
                first_ref[...], back_ref[...], ind_ref[...], sx.at[k],
            )
        return carry

    lax.fori_loop(0, BLOCKS // 2, body, 0)


def gain_kernel(gcm_ref, own_ref, ret_ref, lift_ref, out_ref):
    out_ref[...] = gained(gcm_ref[...], own_ref[...], ret_ref[:, 0, :], lift_ref[...])


def gained(gcm, own, ret, lift):
    m0, m1 = onehots(own)
    ret = ret.astype(BF)
    lane = lax.broadcasted_iota(jnp.int32, (COLS, 256), 1) // 64 % 2
    got = jnp.where(lane == 0, dot(m0, ret, 0, 0), dot(m1, ret, 0, 0)).astype(BF)
    return gcm + dot(got, lift)


def padded_2(x, sides, width):
    for axis, dim in sides:
        size, length = (lax.axis_size(axis), x.shape[dim])
        up = [(i, (i + 1) % size) for i in range(size)]
        down = [(j, i) for i, j in up]
        last = lax.slice_in_dim(x, length - width, length, axis=dim)
        first = lax.slice_in_dim(x, 0, width, axis=dim)
        before = lax.ppermute(last, axis, up)
        after = lax.ppermute(first, axis, down)
        x = jnp.concatenate([before, x, after], axis=dim)
    return x


def call(kernel, shapes, scratch=(), mib=32):
    return pl.pallas_call(
        kernel,
        out_shape=shapes,
        scratch_shapes=list(scratch),
        compiler_params=pltpu.CompilerParams(vmem_limit_bytes=mib * 2**20),
    )


def local(gcm_state, crm_state, owners, ice_mask, horizontal_operator, vertical_inverse, diffusivity):
    t = tables()
    rows_x, rows_y, width = gcm_state.shape
    gcm = gcm_state.reshape(COLS, width)
    own = owners.reshape(1, COLS)
    x = crm_state.reshape(256, 2, 3712).transpose(0, 2, 1).reshape(7424, 128, 2).transpose(0, 2, 1).reshape(14848, 128)
    sds = jax.ShapeDtypeStruct
    out = call(send_kernel, sds((COLS, 1, 384), F32))(
        gcm, own, ice_mask.reshape(COLS, CLEV), t["drive"], t["flag"], t["one"]
    )
    arr = lax.all_to_all(out, ("gx", "gy"), split_axis=0, concat_axis=0, tiled=True)
    new, tend = call(
        cloud_kernel,
        (sds((14848, 128), BF), sds((COLS, 1, 256), F32)),
        [
            pltpu.VMEM((2, 256, 256), BF),
            pltpu.VMEM((2, 256, 256), BF),
            pltpu.VMEM((256, 256), BF),
            pltpu.VMEM((2, ROWS + 8, 128), F32),
        ],
    )(x, arr, horizontal_operator, vertical_inverse, t["tile"], t["rows"], t["first"], t["back"], t["ind"])
    ret = lax.all_to_all(tend, ("gx", "gy"), split_axis=0, concat_axis=0, tiled=True)
    updated = call(gain_kernel, sds((COLS, width), F32))(gcm, own, ret, t["lift"]).reshape(rows_x, rows_y, width)
    padded = padded_2(updated.astype(BF), (("gx", 0), ("gy", 1)), 1).astype(F32)
    neighbours = padded[2:, 1:-1] + padded[:-2, 1:-1] + padded[1:-1, 2:] + padded[1:-1, :-2]
    gcm_out = updated + diffusivity * (neighbours - 4.0 * updated)
    new = new.reshape(7424, 2, 128).transpose(0, 2, 1).reshape(256, 3712, 2).transpose(0, 2, 1)
    return gcm_out, new.reshape(crm_state.shape)


def solution(mesh):
    in_specs = (
        P("gx", "gy", None),
        P(("gx", "gy"), None, None, None, None),
        P(("gx", "gy"), None, None),
        P("gx", "gy", None),
        P(),
        P(),
        P(),
    )
    out_specs = (P("gx", "gy", None), P(("gx", "gy"), None, None, None, None))
    return jax.shard_map(local, mesh=mesh, in_specs=in_specs, out_specs=out_specs, check_vma=False)
```

```python
import jax
import jax.numpy as jnp
from jax import lax
from jax.experimental import pallas as pl
from jax.experimental.pallas import tpu as pltpu
from jax.sharding import PartitionSpec as P

BF, F32 = jnp.bfloat16, jnp.float32
SUBSTEPS, CLEV, CX, LEV, COLS = 4, 58, 64, 72, 128
BLOCKS, GROUP, ROWS = 32, 4, 464
NX, NY, WIDTH = 8, 16, 144
MESH = pl.DeviceIdType.MESH


def iota(shape, dim):
    return lax.broadcasted_iota(jnp.int32, shape, dim)


def level_of(lane):
    place = lane % 64
    return place % 32 * 2 + place // 32


def hat(rows, cols, ratio):
    gap = rows.astype(F32) * ratio - cols.astype(F32)
    return jnp.maximum(0.0, 1.0 - jnp.abs(gap))


def dot(a, b, ca=1, cb=0):
    return lax.dot_general(a, b, (((ca,), (cb,)), ((), ())), preferred_element_type=F32)


def onehots(owners_row, row_owner):
    o, c = iota((COLS, COLS), 0), iota((COLS, COLS), 1)
    same = jnp.where(owners_row == row_owner(o), 1.0, 0.0)
    rank = dot(same.astype(BF), jnp.where(o < c, 1.0, 0.0).astype(BF))
    first = jnp.where(rank < 0.5, same, 0.0)
    return first.astype(BF), (same - first).astype(BF)


def outgoing(gcm, ice, m0, m1):
    low = gcm.astype(BF)
    ice = ice.astype(F32).astype(BF)
    row, lane = iota((WIDTH, 384), 0), iota((WIDTH, 384), 1)
    level = level_of(lane)
    weight = jnp.where(
        (lane // 128 == row // LEV) & (level < CLEV), hat(level, row % LEV, (LEV - 1) / (CLEV - 1)), 0.0
    )
    row2, lane2 = iota((CLEV, 384), 0), iota((CLEV, 384), 1)
    pick = jnp.where((lane2 >= 256) & (level_of(lane2) == row2), 1.0, 0.0)
    lane1 = iota((1, 384), 1)
    drive = dot(low, weight.astype(BF)) + dot(ice, pick.astype(BF)) + jnp.where(lane1 >= 256, 2.0, 0.0)
    drive = drive.astype(BF)
    return jnp.where(iota((COLS, 384), 1) // 64 % 2 == 0, dot(m0, drive), dot(m1, drive)).astype(BF)


def operators(h_ref, v_ref, hb_ref, vb_ref):
    a, b = iota((256, 256), 0) // 64, iota((256, 256), 1) // 64
    diag = a == b
    tile = jnp.where(iota((256, CX), 0) % 64 == iota((256, CX), 1), 1.0, 0.0).astype(BF)
    rows = jnp.where(level_of(iota((256, CLEV), 0)) == iota((256, CLEV), 1), 1.0, 0.0).astype(BF)
    for v in range(2):
        h = (h_ref[v].astype(F32) - 1.0 / 256.0).astype(BF)
        hb_ref[v] = jnp.where(diag, dot(dot(tile, h).astype(BF), tile, 1, 1), 0.0).astype(BF)
    v0 = dot(dot(rows, v_ref[0]).astype(BF), rows, 1, 1)
    v1 = dot(dot(rows, v_ref[1]).astype(BF), rows, 1, 1)
    vb_ref[...] = jnp.where(diag, jnp.where(a < 2, v0, v1), 0.0).astype(BF)


def place():
    return lax.axis_index("gx"), lax.axis_index("gy")


def greet():
    a, b = place()
    barrier = pltpu.get_barrier_semaphore()
    for k in range(1, NX):
        pl.semaphore_signal(barrier, inc=1, device_id=((a + k) % NX, b), device_id_type=MESH)
    for k in range(1, NY):
        pl.semaphore_signal(barrier, inc=1, device_id=(a, (b + k) % NY), device_id_type=MESH)


def greeted():
    pl.semaphore_wait(pltpu.get_barrier_semaphore(), NX + NY - 2)


def swap_x(src, dst, send, recv):
    a, b = place()
    copies = [
        pltpu.make_async_remote_copy(
            src_ref=src.at[(a + k) % NX], dst_ref=dst.at[a], send_sem=send.at[k], recv_sem=recv.at[k],
            device_id=((a + k) % NX, b), device_id_type=MESH,
        )
        for k in range(1, NX)
    ]
    for c in copies:
        c.start()
    dst[a] = src[a]
    return copies


def swap_y(src, dst, send, recv):
    a, b = place()
    copies = [
        pltpu.make_async_remote_copy(
            src_ref=src.at[(b + k) % NY], dst_ref=dst.at[b], send_sem=send.at[k], recv_sem=recv.at[k],
            device_id=(a, (b + k) % NY), device_id_type=MESH,
        )
        for k in range(1, NY)
    ]
    for c in copies:
        c.start()
    dst[b] = src[b]
    return copies


def wait(copies):
    for c in copies:
        c.wait()


def turned(value, rows, cols):
    to, frm = iota((COLS, COLS), 0), iota((COLS, COLS), 1)
    pick = jnp.where((to % rows == frm // cols) & (to // rows == frm % cols), 1.0, 0.0)
    return dot(pick.astype(BF), value)


def out_kernel(
    gcm_ref, own_ref, ice_ref, h_ref, v_ref, arr_ref, hb_ref, vb_ref, a_s, b_s, c_s, d_s, sx_s, rx_s, sy_s, ry_s
):
    greet()
    m0, m1 = onehots(own_ref[...], lambda o: o)
    a_s[...] = outgoing(gcm_ref[...], ice_ref[...], m0, m1).reshape(NX, NY, 384)
    greeted()
    copies = swap_x(a_s, b_s, sx_s, rx_s)
    operators(h_ref, v_ref, hb_ref, vb_ref)
    wait(copies)
    c_s[...] = turned(b_s[...].reshape(COLS, 384), NX, NY).reshape(NY, NX, 384)
    copies = swap_y(c_s, d_s, sy_s, ry_s)
    wait(copies)
    arr_ref[:, 0, :] = turned(d_s[...].reshape(COLS, 384).astype(BF), NY, NX)


def back_kernel(
    gcm_ref, own_ref, tend_ref, diff_ref, out_ref, a_s, b_s, c_s, d_s, u_s, l_s, r_s, hx_s, hy_s, sy0_s,
    sx_s, rx_s, sy_s, ry_s, sh_s, rh_s,
):
    a, b = place()
    greet()
    m0, m1 = onehots(own_ref[...], lambda o: o % NX * NY + o // NX)
    a_s[...] = tend_ref[:, 0, :].astype(BF).reshape(NX, NY, 256)
    greeted()
    copies = swap_x(a_s, b_s, sx_s, rx_s)
    wait(copies)
    c_s[...] = turned(b_s[...].reshape(COLS, 256), NX, NY).reshape(NY, NX, 256)
    copies = swap_y(c_s, d_s, sy_s, ry_s)
    wait(copies)
    got = d_s[...].reshape(COLS, 256).astype(BF)
    lane = iota((COLS, 256), 1) // 64 % 2
    got = jnp.where(lane == 0, dot(m0, got, 0, 0), dot(m1, got, 0, 0)).astype(BF)
    row, col = iota((256, 256), 0), iota((256, 256), 1)
    level = level_of(row)
    grid = jnp.where(col >= LEV, col - LEV, col)
    lift = jnp.where(
        (row // 128 == jnp.where(col >= LEV, 1, 0)) & (level < CLEV) & (col < WIDTH),
        hat(grid, level, (CLEV - 1) / (LEV - 1)),
        0.0,
    )
    gain = dot(got, lift.astype(BF))
    u_s[...] = gain.reshape(NX, NY, 256)
    u_s[:, :, 0:WIDTH] = (gain[:, 0:WIDTH] + gcm_ref[...]).reshape(NX, NY, WIDTH)
    for s in range(2):
        sy0_s[s] = u_s[:, 15 * s, :]
    ends = [
        (u_s.at[NX - 1], hx_s.at[0], ((a + 1) % NX, b)),
        (u_s.at[0], hx_s.at[1], ((a + NX - 1) % NX, b)),
        (sy0_s.at[1], hy_s.at[0], (a, (b + 1) % NY)),
        (sy0_s.at[0], hy_s.at[1], (a, (b + NY - 1) % NY)),
    ]
    copies = [
        pltpu.make_async_remote_copy(
            src_ref=src, dst_ref=dst, send_sem=sh_s.at[i], recv_sem=rh_s.at[i], device_id=dev, device_id_type=MESH
        )
        for i, (src, dst, dev) in enumerate(ends)
    ]
    for c in copies:
        c.start()
    u = u_s[...].reshape(COLS, 256)
    l_s[...] = pltpu.roll(u, 1, 0).reshape(NX, NY, 256)
    r_s[...] = pltpu.roll(u, COLS - 1, 0).reshape(NX, NY, 256)
    wait(copies)
    l_s[:, 0, :] = hy_s[0]
    r_s[:, NY - 1, :] = hy_s[1]
    up = jnp.concatenate([hx_s[0], u[0:112]], axis=0)
    down = jnp.concatenate([u[16:128], hx_s[1]], axis=0)
    total = up + down + (l_s[...] + r_s[...]).reshape(COLS, 256) - 4.0 * u
    out_ref[...] = (u[:, 0:WIDTH] + diff_ref[...] * total[:, 0:WIDTH])


def rolled(a, b, low):
    return jnp.where(low, a, pltpu.roll(b, 64, 1)), jnp.where(low, pltpu.roll(a, 64, 1), b)


def blocks(n, x_ref, arr_ref, hb_ref, vb_ref, out_ref, tend_ref, sx, old_s):
    low = iota((32, 128), 1) < 64
    ind = jnp.where(iota((8, 256), 0) == iota((8, 256), 1) // 64, 1.0, 0.0).astype(BF)
    spread = ind[0:4, :]
    ats = [pl.ds(k * ROWS, ROWS) for k in range(n)]
    state = [[], []]
    forces, flags = [[], []], []
    for k in range(n):
        sx[k, pl.ds(0, ROWS), :] = x_ref[ats[k], :].astype(F32)
    for k in range(n):
        for v in range(2):
            piece = {}
            for j in range(2):
                for h in range(2):
                    d = [sx[k, pl.ds(58 * ((2 * h + i) * 2 + j) + v, 32, stride=2), :] for i in range(2)]
                    piece[j, 0, h], piece[j, 1, h] = rolled(d[0], d[1], low)
            x0 = jnp.concatenate(
                [jnp.concatenate([piece[j, p, 0], piece[j, p, 1]], axis=1) for j in range(2) for p in range(2)], axis=0
            )
            x0 = x0.astype(BF)
            old_s[k, v] = x0
            state[v].append(x0)
    for k in range(n):
        arr = arr_ref[pl.ds(4 * k, 4), 0, :].astype(BF)
        for v in range(2):
            forces[v].append(dot(arr[:, 128 * v : 128 * v + 128], spread, 0, 0) * 0.25)
        flags.append(dot(arr[:, 256:384], spread, 0, 0))
    for step in range(SUBSTEPS):
        f = [dot(jnp.concatenate(state[v], axis=0), hb_ref[v]) for v in range(2)]
        state = [[], []]
        for k in range(n):
            f0 = f[0][k * 128 : (k + 1) * 128] + forces[0][k]
            f1 = f[1][k * 128 : (k + 1) * 128] + forces[1][k]
            e = f1 - 0.5 * f0
            soft = jnp.maximum(e, 0.0) + jnp.log(1.0 + jnp.exp(-jnp.abs(e)))
            q = jnp.where(flags[k] > 2.5, 0.2 * e, 0.4 * soft)
            y = jnp.concatenate([(f0 + 0.5 * q).astype(BF), (f1 - q).astype(BF)], axis=0)
            z = dot(vb_ref[...], y).astype(BF)
            for v in range(2):
                state[v].append(z[v * 128 : (v + 1) * 128])
    for k in range(n):
        old = [old_s[k, v] for v in range(2)]
        diff = jnp.concatenate([(state[v][k].astype(F32) - old[v].astype(F32)).astype(BF) for v in range(2)], axis=0)
        tend = dot(ind, diff, 1, 1) * (1.0 / 64.0)
        tend_ref[pl.ds(4 * k, 4), 0, :] = tend[0:4].astype(BF).astype(F32)
        for v in range(2):
            final = jnp.where(flags[k] > 1.0, state[v][k].astype(F32), old[v].astype(F32))
            for j in range(2):
                for h in range(2):
                    a, b = [
                        final[(j * 2 + p) * 32 : (j * 2 + p + 1) * 32, h * 128 : (h + 1) * 128] for p in range(2)
                    ]
                    d = rolled(a, b, low)
                    for i in range(2):
                        sx[k, pl.ds(58 * ((2 * h + i) * 2 + j) + v, 29, stride=2), :] = d[i][0:29]
        out_ref[ats[k], :] = sx[k, pl.ds(0, ROWS), :].astype(BF)


def cloud_kernel(x_ref, arr_ref, hb_ref, vb_ref, out_ref, tend_ref, sx, old_s):
    sx[:, pl.ds(ROWS, 8), :] = jnp.zeros((GROUP, 8, 128), F32)
    blocks(GROUP, x_ref, arr_ref, hb_ref, vb_ref, out_ref, tend_ref, sx, old_s)


def cloud(x, arr, hb, vb):
    sds = jax.ShapeDtypeStruct
    rows = GROUP * ROWS
    return pl.pallas_call(
        cloud_kernel,
        grid=(BLOCKS // GROUP,),
        in_specs=[
            pl.BlockSpec((rows, 128), lambda t: (t, 0)),
            pl.BlockSpec((4 * GROUP, 1, 384), lambda t: (t, 0, 0)),
            pl.BlockSpec((2, 256, 256), lambda t: (0, 0, 0)),
            pl.BlockSpec((256, 256), lambda t: (0, 0)),
        ],
        out_specs=[
            pl.BlockSpec((rows, 128), lambda t: (t, 0)),
            pl.BlockSpec((4 * GROUP, 1, 256), lambda t: (t, 0, 0)),
        ],
        out_shape=(sds((14848, 128), BF), sds((COLS, 1, 256), F32)),
        scratch_shapes=[
            pltpu.VMEM((GROUP, ROWS + 8, 128), F32),
            pltpu.VMEM((GROUP, 2, 128, 256), BF),
        ],
        compiler_params=pltpu.CompilerParams(vmem_limit_bytes=56 * 2**20),
        name="cloud",
    )(x, arr, hb, vb)


def talk(kernel, shapes, scratch, ident, name, *args):
    dma = pltpu.SemaphoreType.DMA
    return pl.pallas_call(
        kernel,
        out_shape=shapes,
        scratch_shapes=list(scratch) + [dma((NX,)), dma((NX,)), dma((NY,)), dma((NY,))],
        compiler_params=pltpu.CompilerParams(
            collective_id=ident, has_side_effects=True, vmem_limit_bytes=24 * 2**20
        ),
        name=name,
    )(*args)


def local(gcm_state, crm_state, owners, ice_mask, horizontal_operator, vertical_inverse, diffusivity):
    sds, vmem = jax.ShapeDtypeStruct, pltpu.VMEM
    gcm = gcm_state.reshape(COLS, WIDTH)
    own = owners.reshape(1, COLS)
    x = crm_state.reshape(256, 2, 3712).transpose(0, 2, 1).reshape(7424, 128, 2).transpose(0, 2, 1).reshape(14848, 128)
    arr, hb, vb = talk(
        out_kernel,
        (sds((COLS, 1, 384), F32), sds((2, 256, 256), BF), sds((256, 256), BF)),
        [vmem((NX, NY, 384), BF), vmem((NX, NY, 384), BF), vmem((NY, NX, 384), F32), vmem((NY, NX, 384), F32)],
        0, "drive_out",
        gcm, own, ice_mask.reshape(COLS, CLEV), horizontal_operator, vertical_inverse,
    )
    new, tend = cloud(x, arr, hb, vb)
    gcm_out = talk_back(gcm, own, tend, diffusivity.reshape(1, WIDTH))
    new = new.reshape(7424, 2, 128).transpose(0, 2, 1).reshape(256, 3712, 2).transpose(0, 2, 1)
    return gcm_out.reshape(gcm_state.shape), new.reshape(crm_state.shape)


def talk_back(gcm, own, tend, diffusivity):
    sds, vmem, dma = jax.ShapeDtypeStruct, pltpu.VMEM, pltpu.SemaphoreType.DMA
    return pl.pallas_call(
        back_kernel,
        out_shape=sds((COLS, WIDTH), F32),
        scratch_shapes=[
            vmem((NX, NY, 256), BF), vmem((NX, NY, 256), BF), vmem((NY, NX, 256), F32), vmem((NY, NX, 256), F32),
            vmem((NX, NY, 256), F32), vmem((NX, NY, 256), F32), vmem((NX, NY, 256), F32),
            vmem((2, NY, 256), F32), vmem((2, NX, 256), F32), vmem((2, NX, 256), F32),
            dma((NX,)), dma((NX,)), dma((NY,)), dma((NY,)), dma((4,)), dma((4,)),
        ],
        compiler_params=pltpu.CompilerParams(collective_id=1, has_side_effects=True, vmem_limit_bytes=24 * 2**20),
        name="tendency_back",
    )(gcm, own, tend, diffusivity)


def solution(mesh):
    in_specs = (
        P("gx", "gy", None),
        P(("gx", "gy"), None, None, None, None),
        P(("gx", "gy"), None, None),
        P("gx", "gy", None),
        P(),
        P(),
        P(),
    )
    out_specs = (P("gx", "gy", None), P(("gx", "gy"), None, None, None, None))
    return jax.shard_map(local, mesh=mesh, in_specs=in_specs, out_specs=out_specs, check_vma=False)
```

```python
import jax
import jax.numpy as jnp
from jax import lax
from jax.experimental import pallas as pl
from jax.experimental.pallas import tpu as pltpu
from jax.sharding import PartitionSpec as P

BF, F32 = jnp.bfloat16, jnp.float32
SUBSTEPS, CLEV, CX, LEV, COLS = 4, 58, 64, 72, 128
BLOCKS, GROUP, ROWS = 32, 4, 464
NX, NY, WIDTH = 8, 16, 144
VMEM_MIB = 58
MESH = pl.DeviceIdType.MESH


def iota(shape, dim):
    return lax.broadcasted_iota(jnp.int32, shape, dim)


def level_of(lane):
    place = lane % 64
    return place % 32 * 2 + place // 32


def hat(rows, cols, ratio):
    gap = rows.astype(F32) * ratio - cols.astype(F32)
    return jnp.maximum(0.0, 1.0 - jnp.abs(gap))


def dot(a, b, ca=1, cb=0):
    return lax.dot_general(a, b, (((ca,), (cb,)), ((), ())), preferred_element_type=F32)


def onehots(owners_row, row_owner):
    o, c = iota((COLS, COLS), 0), iota((COLS, COLS), 1)
    same = jnp.where(owners_row == row_owner(o), 1.0, 0.0)
    rank = dot(same.astype(BF), jnp.where(o < c, 1.0, 0.0).astype(BF))
    first = jnp.where(rank < 0.5, same, 0.0)
    return first.astype(BF), (same - first).astype(BF)


def outgoing(gcm, ice, m0, m1):
    low = gcm.astype(BF)
    ice = ice.astype(F32).astype(BF)
    row, lane = iota((WIDTH, 384), 0), iota((WIDTH, 384), 1)
    level = level_of(lane)
    weight = jnp.where(
        (lane // 128 == row // LEV) & (level < CLEV), hat(level, row % LEV, (LEV - 1) / (CLEV - 1)), 0.0
    )
    row2, lane2 = iota((CLEV, 384), 0), iota((CLEV, 384), 1)
    pick = jnp.where((lane2 >= 256) & (level_of(lane2) == row2), 1.0, 0.0)
    lane1 = iota((1, 384), 1)
    drive = dot(low, weight.astype(BF)) + dot(ice, pick.astype(BF)) + jnp.where(lane1 >= 256, 2.0, 0.0)
    drive = drive.astype(BF)
    return jnp.where(iota((COLS, 384), 1) // 64 % 2 == 0, dot(m0, drive), dot(m1, drive)).astype(BF)


def operators(h_ref, v_ref, hb_ref, vb_ref):
    a, b = iota((256, 256), 0) // 64, iota((256, 256), 1) // 64
    diag = a == b
    tile = jnp.where(iota((256, CX), 0) % 64 == iota((256, CX), 1), 1.0, 0.0).astype(BF)
    rows = jnp.where(level_of(iota((256, CLEV), 0)) == iota((256, CLEV), 1), 1.0, 0.0).astype(BF)
    for v in range(2):
        h = (h_ref[v].astype(F32) - 1.0 / 256.0).astype(BF)
        hb_ref[v] = jnp.where(diag, dot(dot(tile, h).astype(BF), tile, 1, 1), 0.0).astype(BF)
    v0 = dot(dot(rows, v_ref[0]).astype(BF), rows, 1, 1)
    v1 = dot(dot(rows, v_ref[1]).astype(BF), rows, 1, 1)
    vb_ref[...] = jnp.where(diag, jnp.where(a < 2, v0, v1), 0.0).astype(BF)


def place():
    return lax.axis_index("gx"), lax.axis_index("gy")


def device(index):
    return (index // NY, index % NY)


def rolled(a, b, low):
    return jnp.where(low, a, pltpu.roll(b, 64, 1)), jnp.where(low, pltpu.roll(a, 64, 1), b)


def slot_rows(j, h, i, v, count):
    return pl.ds(58 * ((2 * h + i) * 2 + j) + v, count, stride=2)


def unpack(g, x_s, old_s, sx):
    low = iota((32, 128), 1) < 64
    for k in range(GROUP):
        sx[k, pl.ds(0, ROWS), :] = x_s[g, pl.ds(k * ROWS, ROWS), :].astype(F32)
    for k in range(GROUP):
        for v in range(2):
            piece = {}
            for j in range(2):
                for h in range(2):
                    d = [sx[k, slot_rows(j, h, i, v, 32), :] for i in range(2)]
                    piece[j, 0, h], piece[j, 1, h] = rolled(d[0], d[1], low)
            x0 = jnp.concatenate(
                [jnp.concatenate([piece[j, p, 0], piece[j, p, 1]], axis=1) for j in range(2) for p in range(2)], axis=0
            )
            old_s[g, k, v] = x0.astype(BF)


def evolve(g, arr_s, old_s, hb_s, vb_s, x_s, tend_s, sx):
    low = iota((32, 128), 1) < 64
    ind = jnp.where(iota((8, 256), 0) == iota((8, 256), 1) // 64, 1.0, 0.0).astype(BF)
    spread = ind[0:4, :]
    forces, flags = [[], []], []
    for k in range(GROUP):
        arr = arr_s[pl.ds(g * NY + 4 * k, 4), 0, :].astype(BF)
        for v in range(2):
            forces[v].append(dot(arr[:, 128 * v : 128 * v + 128], spread, 0, 0) * 0.25)
        flags.append(dot(arr[:, 256:384], spread, 0, 0))
    state = [[old_s[g, k, v] for k in range(GROUP)] for v in range(2)]
    for step in range(SUBSTEPS):
        f = [dot(jnp.concatenate(state[v], axis=0), hb_s[v]) for v in range(2)]
        state = [[], []]
        for k in range(GROUP):
            f0 = f[0][k * 128 : (k + 1) * 128] + forces[0][k]
            f1 = f[1][k * 128 : (k + 1) * 128] + forces[1][k]
            e = f1 - 0.5 * f0
            soft = jnp.maximum(e, 0.0) + jnp.log(1.0 + jnp.exp(-jnp.abs(e)))
            q = jnp.where(flags[k] > 2.5, 0.2 * e, 0.4 * soft)
            y = jnp.concatenate([(f0 + 0.5 * q).astype(BF), (f1 - q).astype(BF)], axis=0)
            z = dot(vb_s[...], y).astype(BF)
            for v in range(2):
                state[v].append(z[v * 128 : (v + 1) * 128])
    for k in range(GROUP):
        old = [old_s[g, k, v] for v in range(2)]
        diff = jnp.concatenate([(state[v][k].astype(F32) - old[v].astype(F32)).astype(BF) for v in range(2)], axis=0)
        tend = dot(ind, diff, 1, 1) * (1.0 / 64.0)
        tend_s[pl.ds(g * NY + 4 * k, 4), 0, :] = tend[0:4].astype(BF).astype(F32)
        for v in range(2):
            final = jnp.where(flags[k] > 1.0, state[v][k].astype(F32), old[v].astype(F32))
            for j in range(2):
                for h in range(2):
                    a, b = [
                        final[(j * 2 + p) * 32 : (j * 2 + p + 1) * 32, h * 128 : (h + 1) * 128] for p in range(2)
                    ]
                    d = rolled(a, b, low)
                    for i in range(2):
                        sx[k, slot_rows(j, h, i, v, 29), :] = d[i][0:29]
        x_s[g, pl.ds(k * ROWS, ROWS), :] = sx[k, pl.ds(0, ROWS), :].astype(BF)


def push(src, dst, send, recv, to):
    return pltpu.make_async_remote_copy(
        src_ref=src, dst_ref=dst, send_sem=send, recv_sem=recv, device_id=to, device_id_type=MESH
    )


def settle(ref, sem):
    pltpu.make_async_copy(ref, ref, sem).wait()


def step_kernel(
    gcm_ref, own_ref, ice_ref, h_ref, v_ref, diff_ref, x_hbm, out_ref, crm_hbm,
    x_s, old_s, sx, hb_s, vb_s, send_s, arr_s, tend_s, ret_s, u_s, l_s, r_s, hx_s, hy_s, edge_s,
    load_m, store_m, send_m, arr_m, back_m, ret_m, hs_m, hr_m,
):
    a, b = place()
    me = a * NY + b
    loads = [
        pltpu.make_async_copy(x_hbm.at[pl.ds(g * GROUP * ROWS, GROUP * ROWS)], x_s.at[g], load_m.at[g])
        for g in range(NX)
    ]
    for c in loads:
        c.start()
    barrier = pltpu.get_barrier_semaphore()

    def greet(k, carry):
        pl.semaphore_signal(barrier, inc=1, device_id=device((me + k) % COLS), device_id_type=MESH)
        return carry

    lax.fori_loop(1, COLS, greet, 0, unroll=True)
    m0, m1 = onehots(own_ref[...], lambda o: o)
    send_s[:, 0, :] = outgoing(gcm_ref[...], ice_ref[...], m0, m1).astype(F32)
    sx[:, pl.ds(ROWS, 8), :] = jnp.zeros((GROUP, 8, 128), F32)
    arr_s[pl.ds(me, 1)] = send_s[pl.ds(me, 1)]
    operators(h_ref, v_ref, hb_s, vb_s)
    pl.semaphore_wait(barrier, COLS - 1)

    def spread(g, carry):
        row = (a + 2 * NX - 1 - g) % NX
        for k in range(NY):
            col = (b + k) % NY
            copy = push(send_s.at[row * NY + col], arr_s.at[me], send_m, arr_m.at[a], (row, col))
            if k:
                copy.start()
            else:
                pl.when(g < NX - 1)(copy.start)
        slab = (a + 1 + g) % NX
        settle(x_s.at[slab], load_m.at[slab])
        unpack(slab, x_s, old_s, sx)
        return carry

    lax.fori_loop(0, NX, spread, 0)

    def group(g, carry):
        slab = (a + 1 + g) % NX

        @pl.when(g < NX - 1)
        def _():
            settle(arr_s.at[pl.ds(0, NY)], arr_m.at[slab])

        @pl.when(g == NX - 1)
        def _():
            settle(arr_s.at[pl.ds(0, NY - 1)], arr_m.at[slab])

        evolve(slab, arr_s, old_s, hb_s, vb_s, x_s, tend_s, sx)
        pltpu.make_async_copy(
            x_s.at[slab], crm_hbm.at[pl.ds(pl.multiple_of(slab * GROUP * ROWS, 16), GROUP * ROWS)], store_m.at[slab]
        ).start()
        for k in range(NY):
            col = (b + k) % NY
            copy = push(tend_s.at[slab * NY + col], ret_s.at[me], back_m, ret_m, (slab, col))
            if k:
                copy.start()
            else:
                pl.when(g < NX - 1)(copy.start)
        return carry

    lax.fori_loop(0, NX, group, 0)
    ret_s[pl.ds(me, 1)] = tend_s[pl.ds(me, 1)]
    settle(send_s.at[pl.ds(0, COLS - 1)], send_m)
    row, col = iota((256, 256), 0), iota((256, 256), 1)
    level = level_of(row)
    grid = jnp.where(col >= LEV, col - LEV, col)
    lift = jnp.where(
        (row // 128 == jnp.where(col >= LEV, 1, 0)) & (level < CLEV) & (col < WIDTH),
        hat(grid, level, (CLEV - 1) / (LEV - 1)),
        0.0,
    ).astype(BF)
    lane = iota((COLS, 256), 1) // 64 % 2
    m0, m1 = onehots(own_ref[...], lambda o: o)
    settle(ret_s.at[pl.ds(0, COLS - 1)], ret_m)
    got = ret_s[:, 0, :].astype(BF)
    got = jnp.where(lane == 0, dot(m0, got, 0, 0), dot(m1, got, 0, 0)).astype(BF)
    gain = dot(got, lift)
    u_s[...] = gain.reshape(NX, NY, 256)
    u_s[:, :, 0:WIDTH] = (gain[:, 0:WIDTH] + gcm_ref[...]).reshape(NX, NY, WIDTH)
    for s in range(2):
        edge_s[s] = u_s[:, 15 * s, :]
    ends = [
        (u_s.at[NX - 1], hx_s.at[0], ((a + 1) % NX, b)),
        (u_s.at[0], hx_s.at[1], ((a + NX - 1) % NX, b)),
        (edge_s.at[1], hy_s.at[0], (a, (b + 1) % NY)),
        (edge_s.at[0], hy_s.at[1], (a, (b + NY - 1) % NY)),
    ]
    copies = [push(src, dst, hs_m.at[i], hr_m.at[i], to) for i, (src, dst, to) in enumerate(ends)]
    for c in copies:
        c.start()
    u = u_s[...].reshape(COLS, 256)
    l_s[...] = pltpu.roll(u, 1, 0).reshape(NX, NY, 256)
    r_s[...] = pltpu.roll(u, COLS - 1, 0).reshape(NX, NY, 256)
    settle(tend_s.at[pl.ds(0, COLS - 1)], back_m)
    for g in range(NX):
        settle(x_s.at[g], store_m.at[g])
    for c in copies:
        c.wait()
    l_s[:, 0, :] = hy_s[0]
    r_s[:, NY - 1, :] = hy_s[1]
    up = jnp.concatenate([hx_s[0], u[0:112]], axis=0)
    down = jnp.concatenate([u[16:128], hx_s[1]], axis=0)
    total = up + down + (l_s[...] + r_s[...]).reshape(COLS, 256) - 4.0 * u
    out_ref[...] = u[:, 0:WIDTH] + diff_ref[...] * total[:, 0:WIDTH]


def local(gcm_state, crm_state, owners, ice_mask, horizontal_operator, vertical_inverse, diffusivity):
    sds, vmem, dma = jax.ShapeDtypeStruct, pltpu.VMEM, pltpu.SemaphoreType.DMA
    x = crm_state.reshape(256, 2, 3712).transpose(0, 2, 1).reshape(7424, 128, 2).transpose(0, 2, 1).reshape(14848, 128)
    whole = pl.BlockSpec(memory_space=pltpu.VMEM)
    hbm = pl.BlockSpec(memory_space=pl.ANY)
    gcm_out, new = pl.pallas_call(
        step_kernel,
        in_specs=[whole] * 6 + [hbm],
        out_specs=[whole, hbm],
        out_shape=(sds((COLS, WIDTH), F32), sds((14848, 128), BF)),
        scratch_shapes=[
            vmem((NX, GROUP * ROWS, 128), BF),
            vmem((NX, GROUP, 2, 128, 256), BF),
            vmem((GROUP, ROWS + 8, 128), F32),
            vmem((2, 256, 256), BF),
            vmem((256, 256), BF),
            vmem((COLS, 1, 384), F32),
            vmem((COLS, 1, 384), F32),
            vmem((COLS, 1, 256), F32),
            vmem((COLS, 1, 256), F32),
            vmem((NX, NY, 256), F32),
            vmem((NX, NY, 256), F32),
            vmem((NX, NY, 256), F32),
            vmem((2, NY, 256), F32),
            vmem((2, NX, 256), F32),
            vmem((2, NX, 256), F32),
            dma((NX,)), dma((NX,)), dma, dma((NX,)), dma, dma, dma((4,)), dma((4,)),
        ],
        compiler_params=pltpu.CompilerParams(collective_id=0, has_side_effects=True, vmem_limit_bytes=VMEM_MIB * 2**20),
        name="physics_step",
    )(
        gcm_state.reshape(COLS, WIDTH), owners.reshape(1, COLS), ice_mask.reshape(COLS, CLEV),
        horizontal_operator, vertical_inverse, diffusivity.reshape(1, WIDTH), x,
    )
    new = new.reshape(7424, 2, 128).transpose(0, 2, 1).reshape(256, 3712, 2).transpose(0, 2, 1)
    return gcm_out.reshape(gcm_state.shape), new.reshape(crm_state.shape)


def solution(mesh):
    in_specs = (
        P("gx", "gy", None),
        P(("gx", "gy"), None, None, None, None),
        P(("gx", "gy"), None, None),
        P("gx", "gy", None),
        P(),
        P(),
        P(),
    )
    out_specs = (P("gx", "gy", None), P(("gx", "gy"), None, None, None, None))
    return jax.shard_map(local, mesh=mesh, in_specs=in_specs, out_specs=out_specs, check_vma=False)
```

```python
import jax
import jax.numpy as jnp
from jax import lax
from jax.experimental import pallas as pl
from jax.experimental.pallas import tpu as pltpu
from jax.sharding import PartitionSpec as P

BF, F32 = jnp.bfloat16, jnp.float32
SUBSTEPS, CLEV, CX, LEV, COLS = 4, 58, 64, 72, 128
BLOCKS, GROUP, ROWS = 32, 4, 464
NX, NY, WIDTH = 8, 16, 144
VMEM_MIB = 58
MESH = pl.DeviceIdType.MESH


def iota(shape, dim):
    return lax.broadcasted_iota(jnp.int32, shape, dim)


def level_of(lane):
    place = lane % 64
    return place % 32 * 2 + place // 32


def hat(rows, cols, ratio):
    gap = rows.astype(F32) * ratio - cols.astype(F32)
    return jnp.maximum(0.0, 1.0 - jnp.abs(gap))


def dot(a, b, ca=1, cb=0):
    return lax.dot_general(a, b, (((ca,), (cb,)), ((), ())), preferred_element_type=F32)


def onehots(owners_row, row_owner):
    o, c = iota((COLS, COLS), 0), iota((COLS, COLS), 1)
    same = jnp.where(owners_row == row_owner(o), 1.0, 0.0)
    rank = dot(same.astype(BF), jnp.where(o < c, 1.0, 0.0).astype(BF))
    first = jnp.where(rank < 0.5, same, 0.0)
    return first.astype(BF), (same - first).astype(BF)


def outgoing(gcm, ice, m0, m1):
    low = gcm.astype(BF)
    ice = ice.astype(F32).astype(BF)
    row, lane = iota((WIDTH, 384), 0), iota((WIDTH, 384), 1)
    level = level_of(lane)
    weight = jnp.where(
        (lane // 128 == row // LEV) & (level < CLEV), hat(level, row % LEV, (LEV - 1) / (CLEV - 1)), 0.0
    )
    row2, lane2 = iota((CLEV, 384), 0), iota((CLEV, 384), 1)
    pick = jnp.where((lane2 >= 256) & (level_of(lane2) == row2), 1.0, 0.0)
    lane1 = iota((1, 384), 1)
    drive = dot(low, weight.astype(BF)) + dot(ice, pick.astype(BF)) + jnp.where(lane1 >= 256, 2.0, 0.0)
    drive = drive.astype(BF)
    return jnp.where(iota((COLS, 384), 1) // 64 % 2 == 0, dot(m0, drive), dot(m1, drive)).astype(BF)


def operators(h_ref, v_ref, hb_ref, vb_ref):
    a, b = iota((256, 256), 0) // 64, iota((256, 256), 1) // 64
    diag = a == b
    tile = jnp.where(iota((256, CX), 0) % 64 == iota((256, CX), 1), 1.0, 0.0).astype(BF)
    rows = jnp.where(level_of(iota((256, CLEV), 0)) == iota((256, CLEV), 1), 1.0, 0.0).astype(BF)
    for v in range(2):
        h = (h_ref[v].astype(F32) - 1.0 / 256.0).astype(BF)
        hb_ref[v] = jnp.where(diag, dot(dot(tile, h).astype(BF), tile, 1, 1), 0.0).astype(BF)
    v0 = dot(dot(rows, v_ref[:, 0, :]).astype(BF), rows, 1, 1)
    v1 = dot(dot(rows, v_ref[:, 1, :]).astype(BF), rows, 1, 1)
    vb_ref[...] = jnp.where(diag, jnp.where(a < 2, v0, v1), 0.0).astype(BF)


def place():
    return lax.axis_index("gx"), lax.axis_index("gy")


def device(index):
    return (index // NY, index % NY)


def rolled(a, b, low):
    return jnp.where(low, a, pltpu.roll(b, 64, 1)), jnp.where(low, pltpu.roll(a, 64, 1), b)


def slot_rows(j, h, i, v, count):
    return pl.ds(58 * ((2 * h + i) * 2 + j) + v, count, stride=2)


def unpack(g, x_s, old_s, sx):
    low = iota((32, 128), 1) < 64
    for k in range(GROUP):
        sx[k, pl.ds(0, ROWS), :] = x_s[g, pl.ds(k * ROWS, ROWS), :].astype(F32)
    for k in range(GROUP):
        for v in range(2):
            piece = {}
            for j in range(2):
                for h in range(2):
                    d = [sx[k, slot_rows(j, h, i, v, 32), :] for i in range(2)]
                    piece[j, 0, h], piece[j, 1, h] = rolled(d[0], d[1], low)
            x0 = jnp.concatenate(
                [jnp.concatenate([piece[j, p, 0], piece[j, p, 1]], axis=1) for j in range(2) for p in range(2)], axis=0
            )
            old_s[g, k, v] = x0.astype(BF)


def evolve(g, arr_s, old_s, hb_s, vb_s, x_s, tend_s, sx):
    low = iota((32, 128), 1) < 64
    ind = jnp.where(iota((8, 256), 0) == iota((8, 256), 1) // 64, 1.0, 0.0).astype(BF)
    spread = ind[0:4, :]
    forces, flags = [[], []], []
    for k in range(GROUP):
        arr = arr_s[pl.ds(g * NY + 4 * k, 4), 0, :].astype(BF)
        for v in range(2):
            forces[v].append(dot(arr[:, 128 * v : 128 * v + 128], spread, 0, 0) * 0.25)
        flags.append(dot(arr[:, 256:384], spread, 0, 0))
    state = [[old_s[g, k, v] for k in range(GROUP)] for v in range(2)]
    for step in range(SUBSTEPS):
        f = [dot(jnp.concatenate(state[v], axis=0), hb_s[v]) for v in range(2)]
        state = [[], []]
        for k in range(GROUP):
            f0 = f[0][k * 128 : (k + 1) * 128] + forces[0][k]
            f1 = f[1][k * 128 : (k + 1) * 128] + forces[1][k]
            e = f1 - 0.5 * f0
            soft = jnp.maximum(e, 0.0) + jnp.log(1.0 + jnp.exp(-jnp.abs(e)))
            q = jnp.where(flags[k] > 2.5, 0.2 * e, 0.4 * soft)
            y = jnp.concatenate([(f0 + 0.5 * q).astype(BF), (f1 - q).astype(BF)], axis=0)
            z = dot(vb_s[...], y).astype(BF)
            for v in range(2):
                state[v].append(z[v * 128 : (v + 1) * 128])
    for k in range(GROUP):
        old = [old_s[g, k, v] for v in range(2)]
        diff = jnp.concatenate([(state[v][k].astype(F32) - old[v].astype(F32)).astype(BF) for v in range(2)], axis=0)
        tend = dot(ind, diff, 1, 1) * (1.0 / 64.0)
        tend_s[pl.ds(g * NY + 4 * k, 4), 0, :] = tend[0:4].astype(BF).astype(F32)
        for v in range(2):
            final = jnp.where(flags[k] > 1.0, state[v][k].astype(F32), old[v].astype(F32))
            for j in range(2):
                for h in range(2):
                    a, b = [
                        final[(j * 2 + p) * 32 : (j * 2 + p + 1) * 32, h * 128 : (h + 1) * 128] for p in range(2)
                    ]
                    d = rolled(a, b, low)
                    for i in range(2):
                        sx[k, slot_rows(j, h, i, v, 29), :] = d[i][0:29]
        x_s[g, pl.ds(k * ROWS, ROWS), :] = sx[k, pl.ds(0, ROWS), :].astype(BF)


def push(src, dst, send, recv, to):
    return pltpu.make_async_remote_copy(
        src_ref=src, dst_ref=dst, send_sem=send, recv_sem=recv, device_id=to, device_id_type=MESH
    )


def settle(ref, sem):
    pltpu.make_async_copy(ref, ref, sem).wait()


def step_kernel(
    gcm_ref, own_ref, ice_ref, h_ref, v_ref, diff_ref, x_hbm, out_ref, x_s,
    old_s, sx, hb_s, vb_s, send_s, arr_s, tend_s, ret_s, u_s, l_s, r_s, hx_s, hy_s, edge_s,
    load_m, send_m, arr_m, back_m, ret_m, hs_m, hr_m,
):
    a, b = place()
    me = a * NY + b
    loads = [
        pltpu.make_async_copy(x_hbm.at[pl.ds(g * GROUP * ROWS, GROUP * ROWS)], x_s.at[g], load_m.at[g])
        for g in range(NX)
    ]
    for c in loads:
        c.start()
    barrier = pltpu.get_barrier_semaphore()

    def greet(k, carry):
        pl.semaphore_signal(barrier, inc=1, device_id=device((me + k) % COLS), device_id_type=MESH)
        return carry

    lax.fori_loop(1, COLS, greet, 0, unroll=True)
    m0, m1 = onehots(own_ref[...], lambda o: o)
    send_s[:, 0, :] = outgoing(gcm_ref[...], ice_ref[...], m0, m1).astype(F32)
    sx[:, pl.ds(ROWS, 8), :] = jnp.zeros((GROUP, 8, 128), F32)
    arr_s[pl.ds(me, 1)] = send_s[pl.ds(me, 1)]
    operators(h_ref, v_ref, hb_s, vb_s)
    pl.semaphore_wait(barrier, COLS - 1)

    def spread(g, carry):
        row = (a + 2 * NX - 1 - g) % NX
        for k in range(NY):
            col = (b + k) % NY
            copy = push(send_s.at[row * NY + col], arr_s.at[me], send_m, arr_m.at[a], (row, col))
            if k:
                copy.start()
            else:
                pl.when(g < NX - 1)(copy.start)
        slab = (a + 1 + g) % NX
        settle(x_s.at[slab], load_m.at[slab])
        unpack(slab, x_s, old_s, sx)
        return carry

    lax.fori_loop(0, NX, spread, 0)

    def group(g, carry):
        slab = (a + 1 + g) % NX

        @pl.when(g < NX - 1)
        def _():
            settle(arr_s.at[pl.ds(0, NY)], arr_m.at[slab])

        @pl.when(g == NX - 1)
        def _():
            settle(arr_s.at[pl.ds(0, NY - 1)], arr_m.at[slab])

        evolve(slab, arr_s, old_s, hb_s, vb_s, x_s, tend_s, sx)
        for k in range(NY):
            col = (b + k) % NY
            copy = push(tend_s.at[slab * NY + col], ret_s.at[me], back_m, ret_m, (slab, col))
            if k:
                copy.start()
            else:
                pl.when(g < NX - 1)(copy.start)
        return carry

    lax.fori_loop(0, NX, group, 0)
    ret_s[pl.ds(me, 1)] = tend_s[pl.ds(me, 1)]
    settle(send_s.at[pl.ds(0, COLS - 1)], send_m)
    row, col = iota((256, 256), 0), iota((256, 256), 1)
    level = level_of(row)
    grid = jnp.where(col >= LEV, col - LEV, col)
    lift = jnp.where(
        (row // 128 == jnp.where(col >= LEV, 1, 0)) & (level < CLEV) & (col < WIDTH),
        hat(grid, level, (CLEV - 1) / (LEV - 1)),
        0.0,
    ).astype(BF)
    lane = iota((COLS, 256), 1) // 64 % 2
    m0, m1 = onehots(own_ref[...], lambda o: o)
    settle(ret_s.at[pl.ds(0, COLS - 1)], ret_m)
    got = ret_s[:, 0, :].astype(BF)
    got = jnp.where(lane == 0, dot(m0, got, 0, 0), dot(m1, got, 0, 0)).astype(BF)
    gain = dot(got, lift)
    u_s[...] = gain.reshape(NX, NY, 256)
    u_s[:, :, 0:WIDTH] = (gain[:, 0:WIDTH] + gcm_ref[...]).reshape(NX, NY, WIDTH)
    for s in range(2):
        edge_s[s] = u_s[:, 15 * s, :]
    ends = [
        (u_s.at[NX - 1], hx_s.at[0], ((a + 1) % NX, b)),
        (u_s.at[0], hx_s.at[1], ((a + NX - 1) % NX, b)),
        (edge_s.at[1], hy_s.at[0], (a, (b + 1) % NY)),
        (edge_s.at[0], hy_s.at[1], (a, (b + NY - 1) % NY)),
    ]
    copies = [push(src, dst, hs_m.at[i], hr_m.at[i], to) for i, (src, dst, to) in enumerate(ends)]
    for c in copies:
        c.start()
    u = u_s[...].reshape(COLS, 256)
    l_s[...] = pltpu.roll(u, 1, 0).reshape(NX, NY, 256)
    r_s[...] = pltpu.roll(u, COLS - 1, 0).reshape(NX, NY, 256)
    settle(tend_s.at[pl.ds(0, COLS - 1)], back_m)
    for c in copies:
        c.wait()
    l_s[:, 0, :] = hy_s[0]
    r_s[:, NY - 1, :] = hy_s[1]
    up = jnp.concatenate([hx_s[0], u[0:112]], axis=0)
    down = jnp.concatenate([u[16:128], hx_s[1]], axis=0)
    total = up + down + (l_s[...] + r_s[...]).reshape(COLS, 256) - 4.0 * u
    out_ref[...] = u[:, 0:WIDTH] + diff_ref[...] * total[:, 0:WIDTH]


def local(gcm_state, crm_state, owners, ice_mask, horizontal_operator, vertical_inverse, diffusivity):
    vmem, dma = pltpu.VMEM, pltpu.SemaphoreType.DMA
    x = crm_state.reshape(256, 2, 3712).transpose(0, 2, 1).reshape(7424, 128, 2).transpose(0, 2, 1).reshape(14848, 128)
    whole = pl.BlockSpec(memory_space=pltpu.VMEM)
    hbm = pl.BlockSpec(memory_space=pl.ANY)
    gcm_out, new = pl.pallas_call(
        step_kernel,
        in_specs=[whole] * 6 + [hbm],
        out_specs=[whole, whole],
        out_shape=(vmem((COLS, WIDTH), F32), vmem((NX, GROUP * ROWS, 128), BF)),
        scratch_shapes=[
            vmem((NX, GROUP, 2, 128, 256), BF),
            vmem((GROUP, ROWS + 8, 128), F32),
            vmem((2, 256, 256), BF),
            vmem((256, 256), BF),
            vmem((COLS, 1, 384), F32),
            vmem((COLS, 1, 384), F32),
            vmem((COLS, 1, 256), F32),
            vmem((COLS, 1, 256), F32),
            vmem((NX, NY, 256), F32),
            vmem((NX, NY, 256), F32),
            vmem((NX, NY, 256), F32),
            vmem((2, NY, 256), F32),
            vmem((2, NX, 256), F32),
            vmem((2, NX, 256), F32),
            dma((NX,)), dma, dma((NX,)), dma, dma, dma((4,)), dma((4,)),
        ],
        compiler_params=pltpu.CompilerParams(collective_id=0, has_side_effects=True, vmem_limit_bytes=VMEM_MIB * 2**20),
        name="physics_step",
    )(
        gcm_state.reshape(COLS, WIDTH), owners.reshape(1, COLS), ice_mask.reshape(COLS, CLEV),
        horizontal_operator, vertical_inverse.transpose(1, 0, 2), diffusivity.reshape(1, WIDTH), x,
    )
    new = new.reshape(7424, 2, 128).transpose(0, 2, 1).reshape(256, 3712, 2).transpose(0, 2, 1)
    return gcm_out.reshape(gcm_state.shape), new.reshape(crm_state.shape)


def solution(mesh):
    in_specs = (
        P("gx", "gy", None),
        P(("gx", "gy"), None, None, None, None),
        P(("gx", "gy"), None, None),
        P("gx", "gy", None),
        P(),
        P(),
        P(),
    )
    out_specs = (P("gx", "gy", None), P(("gx", "gy"), None, None, None, None))
    return jax.shard_map(local, mesh=mesh, in_specs=in_specs, out_specs=out_specs, check_vma=False)
```

```python
import jax
import jax.numpy as jnp
from jax import lax
from jax.experimental import pallas as pl
from jax.experimental.pallas import tpu as pltpu
from jax.sharding import PartitionSpec as P

BF, F32 = jnp.bfloat16, jnp.float32
SUBSTEPS, CLEV, CX, LEV, COLS = 4, 58, 64, 72, 128
BLOCKS, GROUP, ROWS, CHAINS = 32, 8, 464, 4
SOURCES, SLABS = 4 * GROUP, BLOCKS // GROUP
NX, NY, WIDTH = 8, 16, 144
VMEM_MIB = 58
HALF, TWICE = (0.5, 1.0), (2.0, 1.0)
LOG2E = 1.4426950408889634
MESH = pl.DeviceIdType.MESH


def iota(shape, dim):
    return lax.broadcasted_iota(jnp.int32, shape, dim)


def level_of(lane):
    place = lane % 64
    return place % 32 * 2 + place // 32


def hat(rows, cols, ratio):
    gap = rows.astype(F32) * ratio - cols.astype(F32)
    return jnp.maximum(0.0, 1.0 - jnp.abs(gap))


def dot(a, b, ca=1, cb=0):
    return lax.dot_general(a, b, (((ca,), (cb,)), ((), ())), preferred_element_type=F32)


def onehots(owners_row, row_owner):
    o, c = iota((COLS, COLS), 0), iota((COLS, COLS), 1)
    same = jnp.where(owners_row == row_owner(o), 1.0, 0.0)
    rank = dot(same.astype(BF), jnp.where(o < c, 1.0, 0.0).astype(BF))
    first = jnp.where(rank < 0.5, same, 0.0)
    return first.astype(BF), (same - first).astype(BF)


def outgoing(gcm, ice, m0, m1):
    low = gcm.astype(BF)
    ice = ice.astype(F32).astype(BF)
    row, lane = iota((WIDTH, 384), 0), iota((WIDTH, 384), 1)
    level = level_of(lane)
    weight = jnp.where(
        (lane // 128 == row // LEV) & (level < CLEV), hat(level, row % LEV, (LEV - 1) / (CLEV - 1)), 0.0
    )
    row2, lane2 = iota((CLEV, 384), 0), iota((CLEV, 384), 1)
    pick = jnp.where((lane2 >= 256) & (level_of(lane2) == row2), 1.0, 0.0)
    lane1 = iota((1, 384), 1)
    drive = dot(low, weight.astype(BF)) + dot(ice, pick.astype(BF)) + jnp.where(lane1 >= 256, 2.0, 0.0)
    drive = drive.astype(BF)
    return jnp.where(iota((COLS, 384), 1) // 64 % 2 == 0, dot(m0, drive), dot(m1, drive)).astype(BF)


def operators(h_ref, v_ref, hb_ref, vb_ref):
    a, b = iota((256, 256), 0) // 64, iota((256, 256), 1) // 64
    diag = a == b
    tile = jnp.where(iota((256, CX), 0) % 64 == iota((256, CX), 1), 1.0, 0.0).astype(BF)
    rows = jnp.where(level_of(iota((256, CLEV), 0)) == iota((256, CLEV), 1), 1.0, 0.0).astype(BF)
    for v in range(2):
        h = (h_ref[v].astype(F32) - 1.0 / 256.0).astype(BF)
        hb_ref[v] = jnp.where(diag, dot(dot(tile, h).astype(BF), tile, 1, 1), 0.0).astype(BF)
    v0 = dot(dot(rows, v_ref[:, 0, :]).astype(BF), rows, 1, 1)
    v1 = dot(dot(rows, v_ref[:, 1, :]).astype(BF), rows, 1, 1)
    vb_ref[...] = jnp.where(diag, jnp.where(a < 2, v0, v1), 0.0).astype(BF)


def place():
    return lax.axis_index("gx"), lax.axis_index("gy")


def device(index):
    return (index // NY, index % NY)


def rolled(a, b, low):
    return jnp.where(low, a, pltpu.roll(b, 64, 1)), jnp.where(low, pltpu.roll(a, 64, 1), b)


def slot_rows(j, h, i, v, count):
    return pl.ds(58 * ((2 * h + i) * 2 + j) + v, count, stride=2)


def unpack(g, x_s, old_s, sx):
    low = iota((32, 128), 1) < 64
    for k in range(GROUP):
        sx[k, pl.ds(0, ROWS), :] = x_s[g, pl.ds(k * ROWS, ROWS), :].astype(F32)
    for k in range(GROUP):
        for v in range(2):
            piece = {}
            for j in range(2):
                for h in range(2):
                    d = [sx[k, slot_rows(j, h, i, v, 32), :] for i in range(2)]
                    piece[j, 0, h], piece[j, 1, h] = rolled(d[0], d[1], low)
            x0 = jnp.concatenate(
                [jnp.concatenate([piece[j, p, 0], piece[j, p, 1]], axis=1) for j in range(2) for p in range(2)], axis=0
            )
            old_s[g, k, v] = (x0 * HALF[v]).astype(BF)


def evolve(g, arr_s, old_s, hb_s, vb_s, x_s, tend_s, sx):
    low = iota((32, 128), 1) < 64
    ind = jnp.where(iota((8, 256), 0) == iota((8, 256), 1) // 64, 1.0, 0.0).astype(BF)
    lane = iota((SOURCES, 384), 1)
    arr = arr_s[pl.ds(g * SOURCES, SOURCES), 0, :]
    arr = jnp.where(lane < 128, 0.125 * arr, jnp.where(lane < 256, 0.25 * arr, arr)).astype(BF)
    pick = iota((SOURCES, 256 * GROUP), 0) == iota((SOURCES, 256 * GROUP), 1) // 64
    wide = dot(arr, jnp.where(pick, 1.0, 0.0).astype(BF), 0, 0)
    forces = [[wide[v * 128 : (v + 1) * 128, k * 256 : (k + 1) * 256] for k in range(GROUP)] for v in range(3)]
    flags = forces[2]
    state = [[old_s[g, k, v] for k in range(GROUP)] for v in range(2)]
    size = GROUP // CHAINS

    def across(c):
        ks = slice(c * size, (c + 1) * size)
        return [dot(jnp.concatenate(state[v][ks], axis=0), hb_s[v]) for v in range(2)]

    def down(c, f):
        for n in range(size):
            k = c * size + n
            f0 = f[0][n * 128 : (n + 1) * 128] + forces[0][k]
            f1 = f[1][n * 128 : (n + 1) * 128] + forces[1][k]
            e = f1 - f0
            soft = jnp.maximum(e, 0.0) + jnp.log(1.0 + jnp.exp2(jnp.abs(e) * -LOG2E))
            q = jnp.where(flags[k] > 2.5, 0.05 * e, 0.1 * soft)
            y = jnp.concatenate([(f0 + q).astype(BF), (f1 - 4.0 * q).astype(BF)], axis=0)
            z = dot(vb_s[...], y).astype(BF)
            for v in range(2):
                state[v][k] = z[v * 128 : (v + 1) * 128]

    held = across(0)
    for turn in range(SUBSTEPS * CHAINS):
        c = turn % CHAINS
        last = turn == SUBSTEPS * CHAINS - 1
        if CHAINS == 1:
            down(0, held)
            held = None if last else across(0)
        else:
            following = None if last else across((c + 1) % CHAINS)
            down(c, held)
            held = following
    for k in range(GROUP):
        old = [old_s[g, k, v] for v in range(2)]
        diff = jnp.concatenate([(state[v][k].astype(F32) - old[v].astype(F32)).astype(BF) for v in range(2)], axis=0)
        tend = dot(ind, diff, 1, 1) * jnp.where(iota((8, 256), 1) < 128, 1.0 / 32.0, 1.0 / 64.0)
        tend_s[pl.ds(g * SOURCES + 4 * k, 4), 0, :] = tend[0:4].astype(BF).astype(F32)
        for v in range(2):
            final = jnp.where(flags[k] > 1.0, state[v][k].astype(F32), old[v].astype(F32)) * TWICE[v]
            for j in range(2):
                for h in range(2):
                    a, b = [
                        final[(j * 2 + p) * 32 : (j * 2 + p + 1) * 32, h * 128 : (h + 1) * 128] for p in range(2)
                    ]
                    d = rolled(a, b, low)
                    for i in range(2):
                        sx[k, slot_rows(j, h, i, v, 29), :] = d[i][0:29]
        x_s[g, pl.ds(k * ROWS, ROWS), :] = sx[k, pl.ds(0, ROWS), :].astype(BF)


def push(src, dst, send, recv, to):
    return pltpu.make_async_remote_copy(
        src_ref=src, dst_ref=dst, send_sem=send, recv_sem=recv, device_id=to, device_id_type=MESH
    )


def settle(ref, sem):
    pltpu.make_async_copy(ref, ref, sem).wait()


def step_kernel(
    gcm_hbm, own_hbm, ice_hbm, h_hbm, v_hbm, diff_hbm, x_hbm, out_ref, x_s,
    gcm_ref, own_ref, ice_ref, h_ref, v_ref, diff_ref, old_s, sx, hb_s, vb_s, send_s, arr_s, tend_s, ret_s, u_s, l_s, r_s, hx_s, hy_s, edge_s,
    small_m, load_m, send_m, arr_m, back_m, ret_m, hs_m, hr_m,
):
    a, b = place()
    me = a * NY + b
    small = [
        pltpu.make_async_copy(src, dst, small_m.at[n])
        for n, (src, dst) in enumerate(
            zip((gcm_hbm, own_hbm, ice_hbm, h_hbm, v_hbm, diff_hbm), (gcm_ref, own_ref, ice_ref, h_ref, v_ref, diff_ref))
        )
    ]
    loads = [
        pltpu.make_async_copy(x_hbm.at[pl.ds(g * GROUP * ROWS, GROUP * ROWS)], x_s.at[g], load_m.at[g])
        for g in range(SLABS)
    ]
    for c in small + loads:
        c.start()
    barrier = pltpu.get_barrier_semaphore()

    def greet(k, carry):
        pl.semaphore_signal(barrier, inc=1, device_id=device((me + k) % COLS), device_id_type=MESH)
        return carry

    lax.fori_loop(1, COLS, greet, 0, unroll=True)
    for c in small:
        c.wait()
    m0, m1 = onehots(own_ref[...], lambda o: o)
    send_s[:, 0, :] = outgoing(gcm_ref[...], ice_ref[...], m0, m1).astype(F32)
    sx[:, pl.ds(ROWS, 8), :] = jnp.zeros((GROUP, 8, 128), F32)
    arr_s[pl.ds(me, 1)] = send_s[pl.ds(me, 1)]
    operators(h_ref, v_ref, hb_s, vb_s)
    pl.semaphore_wait(barrier, COLS - 1)

    def send_drive(g, carry):
        for n in range(2):
            row = (a // 2 + 2 * SLABS - 1 - g) % SLABS * 2 + (a + n) % 2
            for k in range(NY):
                col = (b + k) % NY
                copy = push(send_s.at[row * NY + col], arr_s.at[me], send_m, arr_m.at[a // 2], (row, col))
                if n or k:
                    copy.start()
                else:
                    pl.when(g < SLABS - 1)(copy.start)
        slab = (a // 2 + 1 + g) % SLABS
        settle(x_s.at[slab], load_m.at[slab])
        unpack(slab, x_s, old_s, sx)
        return carry

    lax.fori_loop(0, SLABS, send_drive, 0)

    def group(g, carry):
        slab = (a // 2 + 1 + g) % SLABS

        @pl.when(g < SLABS - 1)
        def _():
            settle(arr_s.at[pl.ds(0, SOURCES)], arr_m.at[slab])

        @pl.when(g == SLABS - 1)
        def _():
            settle(arr_s.at[pl.ds(0, SOURCES - 1)], arr_m.at[slab])

        evolve(slab, arr_s, old_s, hb_s, vb_s, x_s, tend_s, sx)
        for n in range(2):
            row = slab * 2 + (a + n) % 2
            for k in range(NY):
                col = (b + k) % NY
                copy = push(tend_s.at[row * NY + col], ret_s.at[me], back_m, ret_m, (row, col))
                if n or k:
                    copy.start()
                else:
                    pl.when(g < SLABS - 1)(copy.start)
        return carry

    lax.fori_loop(0, SLABS, group, 0)
    ret_s[pl.ds(me, 1)] = tend_s[pl.ds(me, 1)]
    settle(send_s.at[pl.ds(0, COLS - 1)], send_m)
    row, col = iota((256, 256), 0), iota((256, 256), 1)
    level = level_of(row)
    grid = jnp.where(col >= LEV, col - LEV, col)
    lift = jnp.where(
        (row // 128 == jnp.where(col >= LEV, 1, 0)) & (level < CLEV) & (col < WIDTH),
        hat(grid, level, (CLEV - 1) / (LEV - 1)),
        0.0,
    ).astype(BF)
    lane = iota((COLS, 256), 1) // 64 % 2
    m0, m1 = onehots(own_ref[...], lambda o: o)
    settle(ret_s.at[pl.ds(0, COLS - 1)], ret_m)
    got = ret_s[:, 0, :].astype(BF)
    got = jnp.where(lane == 0, dot(m0, got, 0, 0), dot(m1, got, 0, 0)).astype(BF)
    gain = dot(got, lift)
    u_s[...] = gain.reshape(NX, NY, 256)
    u_s[:, :, 0:WIDTH] = (gain[:, 0:WIDTH] + gcm_ref[...]).reshape(NX, NY, WIDTH)
    for s in range(2):
        edge_s[s] = u_s[:, 15 * s, :]
    ends = [
        (u_s.at[NX - 1], hx_s.at[0], ((a + 1) % NX, b)),
        (u_s.at[0], hx_s.at[1], ((a + NX - 1) % NX, b)),
        (edge_s.at[1], hy_s.at[0], (a, (b + 1) % NY)),
        (edge_s.at[0], hy_s.at[1], (a, (b + NY - 1) % NY)),
    ]
    copies = [push(src, dst, hs_m.at[i], hr_m.at[i], to) for i, (src, dst, to) in enumerate(ends)]
    for c in copies:
        c.start()
    u = u_s[...].reshape(COLS, 256)
    l_s[...] = pltpu.roll(u, 1, 0).reshape(NX, NY, 256)
    r_s[...] = pltpu.roll(u, COLS - 1, 0).reshape(NX, NY, 256)
    settle(tend_s.at[pl.ds(0, COLS - 1)], back_m)
    for c in copies:
        c.wait()
    l_s[:, 0, :] = hy_s[0]
    r_s[:, NY - 1, :] = hy_s[1]
    up = jnp.concatenate([hx_s[0], u[0:112]], axis=0)
    down = jnp.concatenate([u[16:128], hx_s[1]], axis=0)
    total = up + down + (l_s[...] + r_s[...]).reshape(COLS, 256) - 4.0 * u
    out_ref[...] = u[:, 0:WIDTH] + diff_ref[...] * total[:, 0:WIDTH]


def local(gcm_state, crm_state, owners, ice_mask, horizontal_operator, vertical_inverse, diffusivity):
    vmem, dma = pltpu.VMEM, pltpu.SemaphoreType.DMA
    x = crm_state.reshape(256, 2, 3712).transpose(0, 2, 1).reshape(7424, 128, 2).transpose(0, 2, 1).reshape(14848, 128)
    whole = pl.BlockSpec(memory_space=pltpu.VMEM)
    hbm = pl.BlockSpec(memory_space=pltpu.HBM)
    gcm_out, new = pl.pallas_call(
        step_kernel,
        in_specs=[hbm] * 7,
        out_specs=[whole, whole],
        out_shape=(vmem((COLS, WIDTH), F32), vmem((SLABS, GROUP * ROWS, 128), BF)),
        scratch_shapes=[
            vmem((COLS, WIDTH), F32), vmem((1, COLS), jnp.int32), vmem((COLS, CLEV), jnp.int32),
            vmem((2, CX, CX), BF), vmem((CLEV, 2, CLEV), BF), vmem((1, WIDTH), F32),
            vmem((SLABS, GROUP, 2, 128, 256), BF),
            vmem((GROUP, ROWS + 8, 128), F32),
            vmem((2, 256, 256), BF),
            vmem((256, 256), BF),
            vmem((COLS, 1, 384), F32),
            vmem((COLS, 1, 384), F32),
            vmem((COLS, 1, 256), F32),
            vmem((COLS, 1, 256), F32),
            vmem((NX, NY, 256), F32),
            vmem((NX, NY, 256), F32),
            vmem((NX, NY, 256), F32),
            vmem((2, NY, 256), F32),
            vmem((2, NX, 256), F32),
            vmem((2, NX, 256), F32),
            dma((6,)), dma((SLABS,)), dma, dma((SLABS,)), dma, dma, dma((4,)), dma((4,)),
        ],
        compiler_params=pltpu.CompilerParams(collective_id=0, has_side_effects=True, vmem_limit_bytes=VMEM_MIB * 2**20),
        name="physics_step",
    )(
        gcm_state.reshape(COLS, WIDTH), owners.reshape(1, COLS), ice_mask.reshape(COLS, CLEV),
        horizontal_operator, vertical_inverse.transpose(1, 0, 2), diffusivity.reshape(1, WIDTH), x,
    )
    new = new.reshape(7424, 2, 128).transpose(0, 2, 1).reshape(256, 3712, 2).transpose(0, 2, 1)
    return gcm_out.reshape(gcm_state.shape), new.reshape(crm_state.shape)


def solution(mesh):
    in_specs = (
        P("gx", "gy", None),
        P(("gx", "gy"), None, None, None, None),
        P(("gx", "gy"), None, None),
        P("gx", "gy", None),
        P(),
        P(),
        P(),
    )
    out_specs = (P("gx", "gy", None), P(("gx", "gy"), None, None, None, None))
    return jax.shard_map(local, mesh=mesh, in_specs=in_specs, out_specs=out_specs, check_vma=False)
```

```python
import jax
import jax.numpy as jnp
from jax import lax
from jax.experimental import pallas as pl
from jax.experimental.pallas import tpu as pltpu
from jax.sharding import PartitionSpec as P

BF, F32 = jnp.bfloat16, jnp.float32
SUBSTEPS, CLEV, CX, LEV, COLS = 4, 58, 64, 72, 128
BLOCKS, GROUP, ROWS, CHAINS = 32, 8, 464, 4
SOURCES, SLABS = 4 * GROUP, BLOCKS // GROUP
NX, NY, WIDTH = 8, 16, 144
VMEM_MIB = 58
HALF, TWICE = (0.5, 1.0), (2.0, 1.0)
LOG2E = 1.4426950408889634
MESH = pl.DeviceIdType.MESH


def iota(shape, dim):
    return lax.broadcasted_iota(jnp.int32, shape, dim)


def level_of(lane):
    place = lane % 64
    return place % 32 * 2 + place // 32


def hat(rows, cols, ratio):
    gap = rows.astype(F32) * ratio - cols.astype(F32)
    return jnp.maximum(0.0, 1.0 - jnp.abs(gap))


def dot(a, b, ca=1, cb=0):
    return lax.dot_general(a, b, (((ca,), (cb,)), ((), ())), preferred_element_type=F32)


def onehots(owners_row, row_owner):
    o, c = iota((COLS, COLS), 0), iota((COLS, COLS), 1)
    same = jnp.where(owners_row == row_owner(o), 1.0, 0.0)
    rank = dot(same.astype(BF), jnp.where(o < c, 1.0, 0.0).astype(BF))
    first = jnp.where(rank < 0.5, same, 0.0)
    return first.astype(BF), (same - first).astype(BF)


def outgoing(gcm, ice, m0, m1):
    low = gcm.astype(BF)
    ice = ice.astype(F32).astype(BF)
    row, lane = iota((WIDTH, 384), 0), iota((WIDTH, 384), 1)
    level = level_of(lane)
    weight = jnp.where(
        (lane // 128 == row // LEV) & (level < CLEV), hat(level, row % LEV, (LEV - 1) / (CLEV - 1)), 0.0
    )
    row2, lane2 = iota((CLEV, 384), 0), iota((CLEV, 384), 1)
    pick = jnp.where((lane2 >= 256) & (level_of(lane2) == row2), 1.0, 0.0)
    lane1 = iota((1, 384), 1)
    drive = dot(low, weight.astype(BF)) + dot(ice, pick.astype(BF)) + jnp.where(lane1 >= 256, 2.0, 0.0)
    drive = drive.astype(BF)
    return jnp.where(iota((COLS, 384), 1) // 64 % 2 == 0, dot(m0, drive), dot(m1, drive)).astype(BF)


def operators(h_ref, v_ref, hb_ref, vb_ref):
    a, b = iota((256, 256), 0) // 64, iota((256, 256), 1) // 64
    diag = a == b
    tile = jnp.where(iota((256, CX), 0) % 64 == iota((256, CX), 1), 1.0, 0.0).astype(BF)
    rows = jnp.where(level_of(iota((256, CLEV), 0)) == iota((256, CLEV), 1), 1.0, 0.0).astype(BF)
    for v in range(2):
        h = (h_ref[v].astype(F32) - 1.0 / 256.0).astype(BF)
        hb_ref[v] = jnp.where(diag, dot(dot(tile, h).astype(BF), tile, 1, 1), 0.0).astype(BF)
    v0 = dot(dot(rows, v_ref[:, 0, :]).astype(BF), rows, 1, 1)
    v1 = dot(dot(rows, v_ref[:, 1, :]).astype(BF), rows, 1, 1)
    vb_ref[...] = jnp.where(diag, jnp.where(a < 2, v0, v1), 0.0).astype(BF)


def place():
    return lax.axis_index("gx"), lax.axis_index("gy")


def device(index):
    return (index // NY, index % NY)


def rolled(a, b, low):
    return jnp.where(low, a, pltpu.roll(b, 64, 1)), jnp.where(low, pltpu.roll(a, 64, 1), b)


def slot_rows(j, h, i, v, count):
    return pl.ds(58 * ((2 * h + i) * 2 + j) + v, count, stride=2)


def unpack(g, x_s, old_s, sx):
    low = iota((32, 128), 1) < 64
    for k in range(GROUP):
        sx[k, pl.ds(0, ROWS), :] = x_s[g, pl.ds(k * ROWS, ROWS), :].astype(F32)
    for k in range(GROUP):
        for v in range(2):
            piece = {}
            for j in range(2):
                for h in range(2):
                    d = [sx[k, slot_rows(j, h, i, v, 32), :] for i in range(2)]
                    piece[j, 0, h], piece[j, 1, h] = rolled(d[0], d[1], low)
            x0 = jnp.concatenate(
                [jnp.concatenate([piece[j, p, 0], piece[j, p, 1]], axis=1) for j in range(2) for p in range(2)], axis=0
            )
            old_s[g, k, v] = (x0 * HALF[v]).astype(BF)


def evolve(g, arr_s, old_s, hb_s, vb_s, x_s, tend_s, sx):
    low = iota((32, 128), 1) < 64
    ind = jnp.where(iota((8, 256), 0) == iota((8, 256), 1) // 64, 1.0, 0.0).astype(BF)
    lane = iota((SOURCES, 384), 1)
    arr = arr_s[pl.ds(g * SOURCES, SOURCES), 0, :]
    arr = jnp.where(lane < 128, 0.125 * arr, jnp.where(lane < 256, 0.25 * arr, arr)).astype(BF)
    pick = iota((SOURCES, 256 * GROUP), 0) == iota((SOURCES, 256 * GROUP), 1) // 64
    wide = dot(arr, jnp.where(pick, 1.0, 0.0).astype(BF), 0, 0)
    forces = [[wide[v * 128 : (v + 1) * 128, k * 256 : (k + 1) * 256] for k in range(GROUP)] for v in range(3)]
    flags = forces[2]
    state = [[old_s[g, k, v] for k in range(GROUP)] for v in range(2)]
    size = GROUP // CHAINS

    def across(c):
        ks = slice(c * size, (c + 1) * size)
        return [dot(jnp.concatenate(state[v][ks], axis=0), hb_s[v]) for v in range(2)]

    def down(c, f):
        for n in range(size):
            k = c * size + n
            f0 = f[0][n * 128 : (n + 1) * 128] + forces[0][k]
            f1 = f[1][n * 128 : (n + 1) * 128] + forces[1][k]
            e = f1 - f0
            soft = jnp.maximum(e, 0.0) + jnp.log(1.0 + jnp.exp2(jnp.abs(e) * -LOG2E))
            q = jnp.where(flags[k] > 2.5, 0.05 * e, 0.1 * soft)
            y = jnp.concatenate([(f0 + q).astype(BF), (f1 - 4.0 * q).astype(BF)], axis=0)
            z = dot(vb_s[...], y).astype(BF)
            for v in range(2):
                state[v][k] = z[v * 128 : (v + 1) * 128]

    held = across(0)
    for turn in range(SUBSTEPS * CHAINS):
        c = turn % CHAINS
        last = turn == SUBSTEPS * CHAINS - 1
        if CHAINS == 1:
            down(0, held)
            held = None if last else across(0)
        else:
            following = None if last else across((c + 1) % CHAINS)
            down(c, held)
            held = following
    half = jnp.where(iota((8, 256), 1) < 128, 1.0 / 32.0, 1.0 / 64.0)
    for k in range(GROUP):
        old = [old_s[g, k, v] for v in range(2)]
        diff = jnp.concatenate([(state[v][k].astype(F32) - old[v].astype(F32)).astype(BF) for v in range(2)], axis=0)
        tend = dot(ind, diff, 1, 1) * half
        tend_s[pl.ds(g * SOURCES + 4 * k, 4), 0, :] = tend[0:4].astype(BF).astype(F32)

    def pack():
        for k in range(GROUP):
            old = [old_s[g, k, v] for v in range(2)]
            for v in range(2):
                final = jnp.where(flags[k] > 1.0, state[v][k].astype(F32), old[v].astype(F32)) * TWICE[v]
                for j in range(2):
                    for h in range(2):
                        a, b = [
                            final[(j * 2 + p) * 32 : (j * 2 + p + 1) * 32, h * 128 : (h + 1) * 128] for p in range(2)
                        ]
                        d = rolled(a, b, low)
                        for i in range(2):
                            sx[k, slot_rows(j, h, i, v, 29), :] = d[i][0:29]
            x_s[g, pl.ds(k * ROWS, ROWS), :] = sx[k, pl.ds(0, ROWS), :].astype(BF)

    return pack


def push(src, dst, send, recv, to):
    return pltpu.make_async_remote_copy(
        src_ref=src, dst_ref=dst, send_sem=send, recv_sem=recv, device_id=to, device_id_type=MESH
    )


def settle(ref, sem):
    pltpu.make_async_copy(ref, ref, sem).wait()


def step_kernel(
    gcm_hbm, own_hbm, ice_hbm, h_hbm, v_hbm, diff_hbm, x_hbm, out_ref, x_s,
    gcm_ref, own_ref, ice_ref, h_ref, v_ref, diff_ref, old_s, sx, hb_s, vb_s, send_s, arr_s, tend_s, ret_s, u_s, l_s, r_s, hx_s, hy_s, edge_s,
    small_m, load_m, send_m, arr_m, back_m, ret_m, hs_m, hr_m,
):
    a, b = place()
    me = a * NY + b
    small = [
        pltpu.make_async_copy(src, dst, small_m.at[n])
        for n, (src, dst) in enumerate(
            zip((gcm_hbm, own_hbm, ice_hbm, h_hbm, v_hbm, diff_hbm), (gcm_ref, own_ref, ice_ref, h_ref, v_ref, diff_ref))
        )
    ]
    loads = [
        pltpu.make_async_copy(x_hbm.at[pl.ds(g * GROUP * ROWS, GROUP * ROWS)], x_s.at[g], load_m.at[g])
        for g in range(SLABS)
    ]
    for c in small + loads:
        c.start()
    barrier = pltpu.get_barrier_semaphore()

    def greet(k, carry):
        pl.semaphore_signal(barrier, inc=1, device_id=device((me + k) % COLS), device_id_type=MESH)
        return carry

    lax.fori_loop(1, COLS, greet, 0, unroll=True)
    for c in small:
        c.wait()
    m0, m1 = onehots(own_ref[...], lambda o: o)
    send_s[:, 0, :] = outgoing(gcm_ref[...], ice_ref[...], m0, m1).astype(F32)
    sx[:, pl.ds(ROWS, 8), :] = jnp.zeros((GROUP, 8, 128), F32)
    arr_s[pl.ds(me, 1)] = send_s[pl.ds(me, 1)]
    pl.semaphore_wait(barrier, COLS - 1)

    def send_drive(g, carry):
        for n in range(2):
            row = (a // 2 + 2 * SLABS - 1 - g) % SLABS * 2 + (a + n) % 2
            for k in range(NY):
                col = (b + k) % NY
                copy = push(send_s.at[row * NY + col], arr_s.at[me], send_m, arr_m.at[a // 2], (row, col))
                if n or k:
                    copy.start()
                else:
                    pl.when(g < SLABS - 1)(copy.start)
        slab = (a // 2 + 1 + g) % SLABS
        settle(x_s.at[slab], load_m.at[slab])
        unpack(slab, x_s, old_s, sx)
        return carry

    lax.fori_loop(0, SLABS, send_drive, 0)
    operators(h_ref, v_ref, hb_s, vb_s)

    def group(g, carry):
        slab = (a // 2 + 1 + g) % SLABS

        @pl.when(g < SLABS - 1)
        def _():
            settle(arr_s.at[pl.ds(0, SOURCES)], arr_m.at[slab])

        @pl.when(g == SLABS - 1)
        def _():
            settle(arr_s.at[pl.ds(0, SOURCES - 1)], arr_m.at[slab])

        pack = evolve(slab, arr_s, old_s, hb_s, vb_s, x_s, tend_s, sx)

        def back(n, k):
            row, col = slab * 2 + (a + n) % 2, (b + k) % NY
            return push(tend_s.at[row * NY + col], ret_s.at[me], back_m, ret_m, (row, col))

        for n in range(2):
            for k in range(NY):
                if n or k:
                    back(n, k).start()
        pack()
        pl.when(g < SLABS - 1)(lambda: back(0, 0).start())
        return carry

    lax.fori_loop(0, SLABS, group, 0)
    ret_s[pl.ds(me, 1)] = tend_s[pl.ds(me, 1)]
    settle(send_s.at[pl.ds(0, COLS - 1)], send_m)
    row, col = iota((256, 256), 0), iota((256, 256), 1)
    level = level_of(row)
    grid = jnp.where(col >= LEV, col - LEV, col)
    lift = jnp.where(
        (row // 128 == jnp.where(col >= LEV, 1, 0)) & (level < CLEV) & (col < WIDTH),
        hat(grid, level, (CLEV - 1) / (LEV - 1)),
        0.0,
    ).astype(BF)
    lane = iota((COLS, 256), 1) // 64 % 2
    m0, m1 = onehots(own_ref[...], lambda o: o)
    settle(ret_s.at[pl.ds(0, COLS - 1)], ret_m)
    got = ret_s[:, 0, :].astype(BF)
    got = jnp.where(lane == 0, dot(m0, got, 0, 0), dot(m1, got, 0, 0)).astype(BF)
    gain = dot(got, lift)
    u_s[...] = gain.reshape(NX, NY, 256)
    u_s[:, :, 0:WIDTH] = (gain[:, 0:WIDTH] + gcm_ref[...]).reshape(NX, NY, WIDTH)
    for s in range(2):
        edge_s[s] = u_s[:, 15 * s, :]
    ends = [
        (u_s.at[NX - 1], hx_s.at[0], ((a + 1) % NX, b)),
        (u_s.at[0], hx_s.at[1], ((a + NX - 1) % NX, b)),
        (edge_s.at[1], hy_s.at[0], (a, (b + 1) % NY)),
        (edge_s.at[0], hy_s.at[1], (a, (b + NY - 1) % NY)),
    ]
    copies = [push(src, dst, hs_m.at[i], hr_m.at[i], to) for i, (src, dst, to) in enumerate(ends)]
    for c in copies:
        c.start()
    u = u_s[...].reshape(COLS, 256)
    l_s[...] = pltpu.roll(u, 1, 0).reshape(NX, NY, 256)
    r_s[...] = pltpu.roll(u, COLS - 1, 0).reshape(NX, NY, 256)
    settle(tend_s.at[pl.ds(0, COLS - 1)], back_m)
    for c in copies:
        c.wait()
    l_s[:, 0, :] = hy_s[0]
    r_s[:, NY - 1, :] = hy_s[1]
    up = jnp.concatenate([hx_s[0], u[0:112]], axis=0)
    down = jnp.concatenate([u[16:128], hx_s[1]], axis=0)
    total = up + down + (l_s[...] + r_s[...]).reshape(COLS, 256) - 4.0 * u
    out_ref[...] = u[:, 0:WIDTH] + diff_ref[...] * total[:, 0:WIDTH]


def local(gcm_state, crm_state, owners, ice_mask, horizontal_operator, vertical_inverse, diffusivity):
    vmem, dma = pltpu.VMEM, pltpu.SemaphoreType.DMA
    x = crm_state.reshape(256, 2, 3712).transpose(0, 2, 1).reshape(7424, 128, 2).transpose(0, 2, 1).reshape(14848, 128)
    whole = pl.BlockSpec(memory_space=pltpu.VMEM)
    hbm = pl.BlockSpec(memory_space=pltpu.HBM)
    gcm_out, new = pl.pallas_call(
        step_kernel,
        in_specs=[hbm] * 7,
        out_specs=[whole, whole],
        out_shape=(vmem((COLS, WIDTH), F32), vmem((SLABS, GROUP * ROWS, 128), BF)),
        scratch_shapes=[
            vmem((COLS, WIDTH), F32), vmem((1, COLS), jnp.int32), vmem((COLS, CLEV), jnp.int32),
            vmem((2, CX, CX), BF), vmem((CLEV, 2, CLEV), BF), vmem((1, WIDTH), F32),
            vmem((SLABS, GROUP, 2, 128, 256), BF),
            vmem((GROUP, ROWS + 8, 128), F32),
            vmem((2, 256, 256), BF),
            vmem((256, 256), BF),
            vmem((COLS, 1, 384), F32),
            vmem((COLS, 1, 384), F32),
            vmem((COLS, 1, 256), F32),
            vmem((COLS, 1, 256), F32),
            vmem((NX, NY, 256), F32),
            vmem((NX, NY, 256), F32),
            vmem((NX, NY, 256), F32),
            vmem((2, NY, 256), F32),
            vmem((2, NX, 256), F32),
            vmem((2, NX, 256), F32),
            dma((6,)), dma((SLABS,)), dma, dma((SLABS,)), dma, dma, dma((4,)), dma((4,)),
        ],
        compiler_params=pltpu.CompilerParams(collective_id=0, has_side_effects=True, vmem_limit_bytes=VMEM_MIB * 2**20),
        name="physics_step",
    )(
        gcm_state.reshape(COLS, WIDTH), owners.reshape(1, COLS), ice_mask.reshape(COLS, CLEV),
        horizontal_operator, vertical_inverse.transpose(1, 0, 2), diffusivity.reshape(1, WIDTH), x,
    )
    new = new.reshape(7424, 2, 128).transpose(0, 2, 1).reshape(256, 3712, 2).transpose(0, 2, 1)
    return gcm_out.reshape(gcm_state.shape), new.reshape(crm_state.shape)


def solution(mesh):
    in_specs = (
        P("gx", "gy", None),
        P(("gx", "gy"), None, None, None, None),
        P(("gx", "gy"), None, None),
        P("gx", "gy", None),
        P(),
        P(),
        P(),
    )
    out_specs = (P("gx", "gy", None), P(("gx", "gy"), None, None, None, None))
    return jax.shard_map(local, mesh=mesh, in_specs=in_specs, out_specs=out_specs, check_vma=False)
```

```python
import jax
import jax.numpy as jnp
from jax import lax
from jax.experimental import pallas as pl
from jax.experimental.pallas import tpu as pltpu
from jax.sharding import PartitionSpec as P

BF, F32 = jnp.bfloat16, jnp.float32
SUBSTEPS, CLEV, CX, LEV, COLS = 4, 58, 64, 72, 128
BLOCKS, GROUP, ROWS, CHAINS = 32, 8, 464, 4
SOURCES, SLABS = 4 * GROUP, BLOCKS // GROUP
NX, NY, WIDTH = 8, 16, 144
VMEM_MIB = 58
HALF, TWICE = (0.5, 1.0), (2.0, 1.0)
LOG2E = 1.4426950408889634
MESH = pl.DeviceIdType.MESH


def iota(shape, dim):
    return lax.broadcasted_iota(jnp.int32, shape, dim)


def level_of(lane):
    place = lane % 64
    return place % 32 * 2 + place // 32


def hat(rows, cols, ratio):
    gap = rows.astype(F32) * ratio - cols.astype(F32)
    return jnp.maximum(0.0, 1.0 - jnp.abs(gap))


def dot(a, b, ca=1, cb=0):
    return lax.dot_general(a, b, (((ca,), (cb,)), ((), ())), preferred_element_type=F32)


def onehots(owners_row, row_owner):
    o, c = iota((COLS, COLS), 0), iota((COLS, COLS), 1)
    same = jnp.where(owners_row == row_owner(o), 1.0, 0.0)
    rank = dot(same.astype(BF), jnp.where(o < c, 1.0, 0.0).astype(BF))
    first = jnp.where(rank < 0.5, same, 0.0)
    return first.astype(BF), (same - first).astype(BF)


def outgoing(gcm, ice, m0, m1):
    low = gcm.astype(BF)
    ice = ice.astype(F32).astype(BF)
    row, lane = iota((WIDTH, 384), 0), iota((WIDTH, 384), 1)
    level = level_of(lane)
    weight = jnp.where(
        (lane // 128 == row // LEV) & (level < CLEV), hat(level, row % LEV, (LEV - 1) / (CLEV - 1)), 0.0
    )
    row2, lane2 = iota((CLEV, 384), 0), iota((CLEV, 384), 1)
    pick = jnp.where((lane2 >= 256) & (level_of(lane2) == row2), 1.0, 0.0)
    lane1 = iota((1, 384), 1)
    drive = dot(low, weight.astype(BF)) + dot(ice, pick.astype(BF)) + jnp.where(lane1 >= 256, 2.0, 0.0)
    drive = drive.astype(BF)
    return jnp.where(iota((COLS, 384), 1) // 64 % 2 == 0, dot(m0, drive), dot(m1, drive)).astype(BF)


def operators(h_ref, v_ref, hb_ref, vb_ref):
    a, b = iota((256, 256), 0) // 64, iota((256, 256), 1) // 64
    diag = a == b
    tile = jnp.where(iota((256, CX), 0) % 64 == iota((256, CX), 1), 1.0, 0.0).astype(BF)
    rows = jnp.where(level_of(iota((256, CLEV), 0)) == iota((256, CLEV), 1), 1.0, 0.0).astype(BF)
    for v in range(2):
        h = (h_ref[v].astype(F32) - 1.0 / 256.0).astype(BF)
        hb_ref[v] = jnp.where(diag, dot(dot(tile, h).astype(BF), tile, 1, 1), 0.0).astype(BF)
    v0 = dot(dot(rows, v_ref[:, 0, :]).astype(BF), rows, 1, 1)
    v1 = dot(dot(rows, v_ref[:, 1, :]).astype(BF), rows, 1, 1)
    vb_ref[...] = jnp.where(diag, jnp.where(a < 2, v0, v1), 0.0).astype(BF)


def place():
    return lax.axis_index("gx"), lax.axis_index("gy")


def device(index):
    return (index // NY, index % NY)


def rolled(a, b, low):
    return jnp.where(low, a, pltpu.roll(b, 64, 1)), jnp.where(low, pltpu.roll(a, 64, 1), b)


def slot_rows(j, h, i, v, count):
    return pl.ds(58 * ((2 * h + i) * 2 + j) + v, count, stride=2)


def unpack(g, x_s, old_s, sx):
    low = iota((32, 128), 1) < 64
    for k in range(GROUP):
        sx[k, pl.ds(0, ROWS), :] = x_s[g, pl.ds(k * ROWS, ROWS), :].astype(F32)
    for k in range(GROUP):
        for v in range(2):
            piece = {}
            for j in range(2):
                for h in range(2):
                    d = [sx[k, slot_rows(j, h, i, v, 32), :] for i in range(2)]
                    piece[j, 0, h], piece[j, 1, h] = rolled(d[0], d[1], low)
            x0 = jnp.concatenate(
                [jnp.concatenate([piece[j, p, 0], piece[j, p, 1]], axis=1) for j in range(2) for p in range(2)], axis=0
            )
            old_s[g, k, v] = (x0 * HALF[v]).astype(BF)


def evolve(g, arr_s, old_s, hb_s, vb_s, x_s, tend_s, sx):
    low = iota((32, 128), 1) < 64
    ind = jnp.where(iota((8, 256), 0) == iota((8, 256), 1) // 64, 1.0, 0.0).astype(BF)
    lane = iota((SOURCES, 384), 1)
    arr = arr_s[pl.ds(g * SOURCES, SOURCES), 0, :]
    arr = jnp.where(lane < 128, 0.125 * arr, jnp.where(lane < 256, 0.25 * arr, arr)).astype(BF)
    pick = iota((SOURCES, 256 * GROUP), 0) == iota((SOURCES, 256 * GROUP), 1) // 64
    wide = dot(arr, jnp.where(pick, 1.0, 0.0).astype(BF), 0, 0)
    forces = [[wide[v * 128 : (v + 1) * 128, k * 256 : (k + 1) * 256] for k in range(GROUP)] for v in range(3)]
    flags = forces[2]
    state = [[old_s[g, k, v] for k in range(GROUP)] for v in range(2)]
    size = GROUP // CHAINS

    def across(c):
        ks = slice(c * size, (c + 1) * size)
        return [dot(jnp.concatenate(state[v][ks], axis=0), hb_s[v]) for v in range(2)]

    def down(c, f):
        for n in range(size):
            k = c * size + n
            f0 = f[0][n * 128 : (n + 1) * 128] + forces[0][k]
            f1 = f[1][n * 128 : (n + 1) * 128] + forces[1][k]
            e = f1 - f0
            soft = jnp.maximum(e, 0.0) + jnp.log(1.0 + jnp.exp2(jnp.abs(e) * -LOG2E))
            q = jnp.where(flags[k] > 2.5, 0.05 * e, 0.1 * soft)
            y = jnp.concatenate([(f0 + q).astype(BF), (f1 - 4.0 * q).astype(BF)], axis=0)
            z = dot(vb_s[...], y).astype(BF)
            for v in range(2):
                state[v][k] = z[v * 128 : (v + 1) * 128]

    held = across(0)
    for turn in range(SUBSTEPS * CHAINS):
        c = turn % CHAINS
        last = turn == SUBSTEPS * CHAINS - 1
        if CHAINS == 1:
            down(0, held)
            held = None if last else across(0)
        else:
            following = None if last else across((c + 1) % CHAINS)
            down(c, held)
            held = following
    half = jnp.where(iota((8, 256), 1) < 128, 1.0 / 32.0, 1.0 / 64.0)
    for k in range(GROUP):
        old = [old_s[g, k, v] for v in range(2)]
        diff = jnp.concatenate([(state[v][k].astype(F32) - old[v].astype(F32)).astype(BF) for v in range(2)], axis=0)
        tend = dot(ind, diff, 1, 1) * half
        tend_s[pl.ds(g * SOURCES + 4 * k, 4), 0, :] = tend[0:4].astype(BF).astype(F32)

    def pack():
        for k in range(GROUP):
            old = [old_s[g, k, v] for v in range(2)]
            for v in range(2):
                final = jnp.where(flags[k] > 1.0, state[v][k].astype(F32), old[v].astype(F32)) * TWICE[v]
                for j in range(2):
                    for h in range(2):
                        a, b = [
                            final[(j * 2 + p) * 32 : (j * 2 + p + 1) * 32, h * 128 : (h + 1) * 128] for p in range(2)
                        ]
                        d = rolled(a, b, low)
                        for i in range(2):
                            sx[k, slot_rows(j, h, i, v, 29), :] = d[i][0:29]
            x_s[g, pl.ds(k * ROWS, ROWS), :] = sx[k, pl.ds(0, ROWS), :].astype(BF)

    return pack


def push(src, dst, send, recv, to):
    return pltpu.make_async_remote_copy(
        src_ref=src, dst_ref=dst, send_sem=send, recv_sem=recv, device_id=to, device_id_type=MESH
    )


def settle(ref, sem):
    pltpu.make_async_copy(ref, ref, sem).wait()


def step_kernel(
    gcm_hbm, own_hbm, ice_hbm, h_hbm, v_hbm, diff_hbm, x_hbm, out_ref, x_s,
    gcm_ref, own_ref, ice_ref, h_ref, v_ref, diff_ref, old_s, sx, hb_s, vb_s, send_s, arr_s, tend_s, ret_s, u_s, l_s, r_s, hx_s, hy_s, edge_s,
    row_m, small_m, load_m, send_m, arr_m, back_m, ret_m, hs_m, hr_m,
):
    a, b = place()
    me = a * NY + b
    small = [
        pltpu.make_async_copy(src, dst, small_m.at[n])
        for n, (src, dst) in enumerate(
            zip((gcm_hbm, own_hbm, ice_hbm, h_hbm, v_hbm, diff_hbm), (gcm_ref, own_ref, ice_ref, h_ref, v_ref, diff_ref))
        )
    ]
    loads = [
        pltpu.make_async_copy(x_hbm.at[pl.ds(g * GROUP * ROWS, GROUP * ROWS)], x_s.at[g], load_m.at[g])
        for g in range(SLABS)
    ]
    for c in small + loads:
        c.start()
    barrier = pltpu.get_barrier_semaphore()

    along_x = [(lax.rem(a + k, NX), b) for k in range(1, NX)]
    along_y = [(a, lax.rem(b + k, NY)) for k in range(1, NY)]
    for to in along_x + along_y:
        pl.semaphore_signal(barrier, inc=1, device_id=to, device_id_type=MESH)
    for c in small:
        c.wait()
    m0, m1 = onehots(own_ref[...], lambda o: o)
    send_s[:, 0, :] = outgoing(gcm_ref[...], ice_ref[...], m0, m1).astype(F32)
    sx[:, pl.ds(ROWS, 8), :] = jnp.zeros((GROUP, 8, 128), F32)
    arr_s[pl.ds(me, 1)] = send_s[pl.ds(me, 1)]
    pl.semaphore_wait(barrier, NX + NY - 2)
    for to in along_x:
        pl.semaphore_signal(row_m, inc=1, device_id=to, device_id_type=MESH)
    pl.semaphore_wait(row_m, NX - 1)

    def send_drive(g, carry):
        for n in range(2):
            row = (a // 2 + 2 * SLABS - 1 - g) % SLABS * 2 + (a + n) % 2
            for k in range(NY):
                col = (b + k) % NY
                copy = push(send_s.at[row * NY + col], arr_s.at[me], send_m, arr_m.at[a // 2], (row, col))
                if n or k:
                    copy.start()
                else:
                    pl.when(g < SLABS - 1)(copy.start)
        slab = (a // 2 + 1 + g) % SLABS
        settle(x_s.at[slab], load_m.at[slab])
        unpack(slab, x_s, old_s, sx)
        return carry

    lax.fori_loop(0, SLABS, send_drive, 0)
    operators(h_ref, v_ref, hb_s, vb_s)

    def group(g, carry):
        slab = (a // 2 + 1 + g) % SLABS

        @pl.when(g < SLABS - 1)
        def _():
            settle(arr_s.at[pl.ds(0, SOURCES)], arr_m.at[slab])

        @pl.when(g == SLABS - 1)
        def _():
            settle(arr_s.at[pl.ds(0, SOURCES - 1)], arr_m.at[slab])

        pack = evolve(slab, arr_s, old_s, hb_s, vb_s, x_s, tend_s, sx)

        def back(n, k):
            row, col = slab * 2 + (a + n) % 2, (b + k) % NY
            return push(tend_s.at[row * NY + col], ret_s.at[me], back_m, ret_m, (row, col))

        for n in range(2):
            for k in range(NY):
                if n or k:
                    back(n, k).start()
        pack()
        pl.when(g < SLABS - 1)(lambda: back(0, 0).start())
        return carry

    lax.fori_loop(0, SLABS, group, 0)
    ret_s[pl.ds(me, 1)] = tend_s[pl.ds(me, 1)]
    settle(send_s.at[pl.ds(0, COLS - 1)], send_m)
    row, col = iota((256, 256), 0), iota((256, 256), 1)
    level = level_of(row)
    grid = jnp.where(col >= LEV, col - LEV, col)
    lift = jnp.where(
        (row // 128 == jnp.where(col >= LEV, 1, 0)) & (level < CLEV) & (col < WIDTH),
        hat(grid, level, (CLEV - 1) / (LEV - 1)),
        0.0,
    ).astype(BF)
    lane = iota((COLS, 256), 1) // 64 % 2
    m0, m1 = onehots(own_ref[...], lambda o: o)
    settle(ret_s.at[pl.ds(0, COLS - 1)], ret_m)
    got = ret_s[:, 0, :].astype(BF)
    got = jnp.where(lane == 0, dot(m0, got, 0, 0), dot(m1, got, 0, 0)).astype(BF)
    gain = dot(got, lift)
    u_s[...] = gain.reshape(NX, NY, 256)
    u_s[:, :, 0:WIDTH] = (gain[:, 0:WIDTH] + gcm_ref[...]).reshape(NX, NY, WIDTH)
    for s in range(2):
        edge_s[s] = u_s[:, 15 * s, :]
    ends = [
        (u_s.at[NX - 1], hx_s.at[0], ((a + 1) % NX, b)),
        (u_s.at[0], hx_s.at[1], ((a + NX - 1) % NX, b)),
        (edge_s.at[1], hy_s.at[0], (a, (b + 1) % NY)),
        (edge_s.at[0], hy_s.at[1], (a, (b + NY - 1) % NY)),
    ]
    copies = [push(src, dst, hs_m.at[i], hr_m.at[i], to) for i, (src, dst, to) in enumerate(ends)]
    for c in copies:
        c.start()
    u = u_s[...].reshape(COLS, 256)
    l_s[...] = pltpu.roll(u, 1, 0).reshape(NX, NY, 256)
    r_s[...] = pltpu.roll(u, COLS - 1, 0).reshape(NX, NY, 256)
    settle(tend_s.at[pl.ds(0, COLS - 1)], back_m)
    for c in copies:
        c.wait()
    l_s[:, 0, :] = hy_s[0]
    r_s[:, NY - 1, :] = hy_s[1]
    up = jnp.concatenate([hx_s[0], u[0:112]], axis=0)
    down = jnp.concatenate([u[16:128], hx_s[1]], axis=0)
    total = up + down + (l_s[...] + r_s[...]).reshape(COLS, 256) - 4.0 * u
    out_ref[...] = u[:, 0:WIDTH] + diff_ref[...] * total[:, 0:WIDTH]


def local(gcm_state, crm_state, owners, ice_mask, horizontal_operator, vertical_inverse, diffusivity):
    vmem, dma = pltpu.VMEM, pltpu.SemaphoreType.DMA
    x = crm_state.reshape(256, 2, 3712).transpose(0, 2, 1).reshape(7424, 128, 2).transpose(0, 2, 1).reshape(14848, 128)
    whole = pl.BlockSpec(memory_space=pltpu.VMEM)
    hbm = pl.BlockSpec(memory_space=pltpu.HBM)
    gcm_out, new = pl.pallas_call(
        step_kernel,
        in_specs=[hbm] * 7,
        out_specs=[whole, whole],
        out_shape=(vmem((COLS, WIDTH), F32), vmem((SLABS, GROUP * ROWS, 128), BF)),
        scratch_shapes=[
            vmem((COLS, WIDTH), F32), vmem((1, COLS), jnp.int32), vmem((COLS, CLEV), jnp.int32),
            vmem((2, CX, CX), BF), vmem((CLEV, 2, CLEV), BF), vmem((1, WIDTH), F32),
            vmem((SLABS, GROUP, 2, 128, 256), BF),
            vmem((GROUP, ROWS + 8, 128), F32),
            vmem((2, 256, 256), BF),
            vmem((256, 256), BF),
            vmem((COLS, 1, 384), F32),
            vmem((COLS, 1, 384), F32),
            vmem((COLS, 1, 256), F32),
            vmem((COLS, 1, 256), F32),
            vmem((NX, NY, 256), F32),
            vmem((NX, NY, 256), F32),
            vmem((NX, NY, 256), F32),
            vmem((2, NY, 256), F32),
            vmem((2, NX, 256), F32),
            vmem((2, NX, 256), F32),
            pltpu.SemaphoreType.REGULAR, dma((6,)), dma((SLABS,)), dma, dma((SLABS,)), dma, dma, dma((4,)), dma((4,)),
        ],
        compiler_params=pltpu.CompilerParams(collective_id=0, has_side_effects=True, vmem_limit_bytes=VMEM_MIB * 2**20),
        name="physics_step",
    )(
        gcm_state.reshape(COLS, WIDTH), owners.reshape(1, COLS), ice_mask.reshape(COLS, CLEV),
        horizontal_operator, vertical_inverse.transpose(1, 0, 2), diffusivity.reshape(1, WIDTH), x,
    )
    new = new.reshape(7424, 2, 128).transpose(0, 2, 1).reshape(256, 3712, 2).transpose(0, 2, 1)
    return gcm_out.reshape(gcm_state.shape), new.reshape(crm_state.shape)


def solution(mesh):
    in_specs = (
        P("gx", "gy", None),
        P(("gx", "gy"), None, None, None, None),
        P(("gx", "gy"), None, None),
        P("gx", "gy", None),
        P(),
        P(),
        P(),
    )
    out_specs = (P("gx", "gy", None), P(("gx", "gy"), None, None, None, None))
    return jax.shard_map(local, mesh=mesh, in_specs=in_specs, out_specs=out_specs, check_vma=False)
```

```python
import jax
import jax.numpy as jnp
from jax import lax
from jax.experimental import pallas as pl
from jax.experimental.pallas import tpu as pltpu
from jax.sharding import PartitionSpec as P

BF, F32 = jnp.bfloat16, jnp.float32
SUBSTEPS, CLEV, CX, LEV, COLS = 4, 58, 64, 72, 128
BLOCKS, GROUP, ROWS, CHAINS = 32, 8, 464, 4
SOURCES, SLABS = 4 * GROUP, BLOCKS // GROUP
NX, NY, WIDTH = 8, 16, 144
VMEM_MIB = 58
HALF, TWICE = (0.5, 1.0), (2.0, 1.0)
LOG2E = 1.4426950408889634
MESH = pl.DeviceIdType.MESH


def iota(shape, dim):
    return lax.broadcasted_iota(jnp.int32, shape, dim)


def level_of(lane):
    place = lane % 64
    return place % 32 * 2 + place // 32


def hat(rows, cols, ratio):
    gap = rows.astype(F32) * ratio - cols.astype(F32)
    return jnp.maximum(0.0, 1.0 - jnp.abs(gap))


def dot(a, b, ca=1, cb=0):
    return lax.dot_general(a, b, (((ca,), (cb,)), ((), ())), preferred_element_type=F32)


def onehots(owners_row, row_owner):
    o, c = iota((COLS, COLS), 0), iota((COLS, COLS), 1)
    same = jnp.where(owners_row == row_owner(o), 1.0, 0.0)
    rank = dot(same.astype(BF), jnp.where(o < c, 1.0, 0.0).astype(BF))
    first = jnp.where(rank < 0.5, same, 0.0)
    return first.astype(BF), (same - first).astype(BF)


def outgoing(gcm, ice, m0, m1):
    low = gcm.astype(BF)
    ice = ice.astype(F32).astype(BF)
    row, lane = iota((WIDTH, 384), 0), iota((WIDTH, 384), 1)
    level = level_of(lane)
    weight = jnp.where(
        (lane // 128 == row // LEV) & (level < CLEV), hat(level, row % LEV, (LEV - 1) / (CLEV - 1)), 0.0
    )
    row2, lane2 = iota((CLEV, 384), 0), iota((CLEV, 384), 1)
    pick = jnp.where((lane2 >= 256) & (level_of(lane2) == row2), 1.0, 0.0)
    lane1 = iota((1, 384), 1)
    drive = dot(low, weight.astype(BF)) + dot(ice, pick.astype(BF)) + jnp.where(lane1 >= 256, 2.0, 0.0)
    drive = drive.astype(BF)
    return jnp.where(iota((COLS, 384), 1) // 64 % 2 == 0, dot(m0, drive), dot(m1, drive)).astype(BF)


def operators(h_ref, v_ref, hb_ref, vb_ref):
    a, b = iota((256, 256), 0) // 64, iota((256, 256), 1) // 64
    diag = a == b
    tile = jnp.where(iota((256, CX), 0) % 64 == iota((256, CX), 1), 1.0, 0.0).astype(BF)
    rows = jnp.where(level_of(iota((256, CLEV), 0)) == iota((256, CLEV), 1), 1.0, 0.0).astype(BF)
    for v in range(2):
        h = (h_ref[v].astype(F32) - 1.0 / 256.0).astype(BF)
        hb_ref[v] = jnp.where(diag, dot(dot(tile, h).astype(BF), tile, 1, 1), 0.0).astype(BF)
    v0 = dot(dot(rows, v_ref[:, 0, :]).astype(BF), rows, 1, 1)
    v1 = dot(dot(rows, v_ref[:, 1, :]).astype(BF), rows, 1, 1)
    vb_ref[...] = jnp.where(diag, jnp.where(a < 2, v0, v1), 0.0).astype(BF)


def place():
    return lax.axis_index("gx"), lax.axis_index("gy")


def device(index):
    return (index // NY, index % NY)


def rolled(a, b, low):
    return jnp.where(low, a, pltpu.roll(b, 64, 1)), jnp.where(low, pltpu.roll(a, 64, 1), b)


def slot_rows(j, h, i, v, count):
    return pl.ds(58 * ((2 * h + i) * 2 + j) + v, count, stride=2)


def unpack(g, x_s, old_s, sx):
    low = iota((32, 128), 1) < 64
    for k in range(GROUP):
        sx[k, pl.ds(0, ROWS), :] = x_s[g, pl.ds(k * ROWS, ROWS), :].astype(F32)
    for k in range(GROUP):
        for v in range(2):
            piece = {}
            for j in range(2):
                for h in range(2):
                    d = [sx[k, slot_rows(j, h, i, v, 32), :] for i in range(2)]
                    piece[j, 0, h], piece[j, 1, h] = rolled(d[0], d[1], low)
            x0 = jnp.concatenate(
                [jnp.concatenate([piece[j, p, 0], piece[j, p, 1]], axis=1) for j in range(2) for p in range(2)], axis=0
            )
            old_s[g, k, v] = (x0 * HALF[v]).astype(BF)


def evolve(g, arr_s, old_s, hb_s, vb_s, x_s, tend_s, sx):
    low = iota((32, 128), 1) < 64
    ind = jnp.where(iota((8, 256), 0) == iota((8, 256), 1) // 64, 1.0, 0.0).astype(BF)
    lane = iota((SOURCES, 384), 1)
    arr = arr_s[pl.ds(g * SOURCES, SOURCES), 0, :]
    arr = jnp.where(lane < 128, 0.125 * arr, jnp.where(lane < 256, 0.25 * arr, arr)).astype(BF)
    pick = iota((SOURCES, 256 * GROUP), 0) == iota((SOURCES, 256 * GROUP), 1) // 64
    wide = dot(arr, jnp.where(pick, 1.0, 0.0).astype(BF), 0, 0)
    forces = [[wide[v * 128 : (v + 1) * 128, k * 256 : (k + 1) * 256] for k in range(GROUP)] for v in range(3)]
    flags = forces[2]
    state = [[old_s[g, k, v] for k in range(GROUP)] for v in range(2)]
    size = GROUP // CHAINS

    def across(c):
        ks = slice(c * size, (c + 1) * size)
        return [dot(jnp.concatenate(state[v][ks], axis=0), hb_s[v]) for v in range(2)]

    def down(c, f):
        for n in range(size):
            k = c * size + n
            f0 = f[0][n * 128 : (n + 1) * 128] + forces[0][k]
            f1 = f[1][n * 128 : (n + 1) * 128] + forces[1][k]
            e = f1 - f0
            soft = jnp.maximum(e, 0.0) + jnp.log(1.0 + jnp.exp2(jnp.abs(e) * -LOG2E))
            q = jnp.where(flags[k] > 2.5, 0.05 * e, 0.1 * soft)
            y = jnp.concatenate([(f0 + q).astype(BF), (f1 - 4.0 * q).astype(BF)], axis=0)
            z = dot(vb_s[...], y).astype(BF)
            for v in range(2):
                state[v][k] = z[v * 128 : (v + 1) * 128]

    held = across(0)
    for turn in range(SUBSTEPS * CHAINS):
        c = turn % CHAINS
        last = turn == SUBSTEPS * CHAINS - 1
        if CHAINS == 1:
            down(0, held)
            held = None if last else across(0)
        else:
            following = None if last else across((c + 1) % CHAINS)
            down(c, held)
            held = following
    half = jnp.where(iota((8, 256), 1) < 128, 1.0 / 32.0, 1.0 / 64.0)
    for k in range(GROUP):
        old = [old_s[g, k, v] for v in range(2)]
        diff = jnp.concatenate([(state[v][k].astype(F32) - old[v].astype(F32)).astype(BF) for v in range(2)], axis=0)
        tend = dot(ind, diff, 1, 1) * half
        tend_s[pl.ds(g * SOURCES + 4 * k, 4), 0, :] = tend[0:4].astype(BF).astype(F32)

    def pack():
        for k in range(GROUP):
            old = [old_s[g, k, v] for v in range(2)]
            for v in range(2):
                final = jnp.where(flags[k] > 1.0, state[v][k].astype(F32), old[v].astype(F32)) * TWICE[v]
                for j in range(2):
                    for h in range(2):
                        a, b = [
                            final[(j * 2 + p) * 32 : (j * 2 + p + 1) * 32, h * 128 : (h + 1) * 128] for p in range(2)
                        ]
                        d = rolled(a, b, low)
                        for i in range(2):
                            sx[k, slot_rows(j, h, i, v, 29), :] = d[i][0:29]
            x_s[g, pl.ds(k * ROWS, ROWS), :] = sx[k, pl.ds(0, ROWS), :].astype(BF)

    return pack


def push(src, dst, send, recv, to):
    return pltpu.make_async_remote_copy(
        src_ref=src, dst_ref=dst, send_sem=send, recv_sem=recv, device_id=to, device_id_type=MESH
    )


def settle(ref, sem):
    pltpu.make_async_copy(ref, ref, sem).wait()


def step_kernel(
    gcm_hbm, own_hbm, ice_hbm, h_hbm, v_hbm, diff_hbm, x_hbm, out_ref, x_s,
    gcm_ref, own_ref, ice_ref, h_ref, v_ref, diff_ref, old_s, sx, hb_s, vb_s, send_s, arr_s, tend_s, ret_s, u_s, l_s, r_s, hx_s, hy_s, edge_s,
    row_m, small_m, load_m, send_m, arr_m, back_m, ret_m, hs_m, hr_m,
):
    a, b = place()
    me = a * NY + b
    small = [
        pltpu.make_async_copy(src, dst, small_m.at[n])
        for n, (src, dst) in enumerate(
            zip((gcm_hbm, own_hbm, ice_hbm, h_hbm, v_hbm, diff_hbm), (gcm_ref, own_ref, ice_ref, h_ref, v_ref, diff_ref))
        )
    ]
    loads = [
        pltpu.make_async_copy(x_hbm.at[pl.ds(g * GROUP * ROWS, GROUP * ROWS)], x_s.at[g], load_m.at[g])
        for g in range(SLABS)
    ]
    for c in small + loads:
        c.start()
    barrier = pltpu.get_barrier_semaphore()

    along_x = [(lax.rem(a + k, NX), b) for k in range(1, NX)]
    along_y = [(a, lax.rem(b + k, NY)) for k in range(1, NY)]
    for to in along_x + along_y:
        pl.semaphore_signal(barrier, inc=1, device_id=to, device_id_type=MESH)
    pl.semaphore_wait(barrier, NX + NY - 2)
    for to in along_x:
        pl.semaphore_signal(row_m, inc=1, device_id=to, device_id_type=MESH)
    for c in small:
        c.wait()
    m0, m1 = onehots(own_ref[...], lambda o: o)
    send_s[:, 0, :] = outgoing(gcm_ref[...], ice_ref[...], m0, m1).astype(F32)
    sx[:, pl.ds(ROWS, 8), :] = jnp.zeros((GROUP, 8, 128), F32)
    arr_s[pl.ds(me, 1)] = send_s[pl.ds(me, 1)]
    pl.semaphore_wait(row_m, NX - 1)

    def send_drive(g, carry):
        for n in range(2):
            row = (a // 2 + 2 * SLABS - 1 - g) % SLABS * 2 + (a + n) % 2
            for k in range(NY):
                col = (b + k) % NY
                copy = push(send_s.at[row * NY + col], arr_s.at[me], send_m, arr_m.at[a // 2], (row, col))
                if n or k:
                    copy.start()
                else:
                    pl.when(g < SLABS - 1)(copy.start)
        slab = (a // 2 + 1 + g) % SLABS
        settle(x_s.at[slab], load_m.at[slab])
        unpack(slab, x_s, old_s, sx)
        return carry

    lax.fori_loop(0, SLABS, send_drive, 0)
    operators(h_ref, v_ref, hb_s, vb_s)

    def group(g, carry):
        slab = (a // 2 + 1 + g) % SLABS

        @pl.when(g < SLABS - 1)
        def _():
            settle(arr_s.at[pl.ds(0, SOURCES)], arr_m.at[slab])

        @pl.when(g == SLABS - 1)
        def _():
            settle(arr_s.at[pl.ds(0, SOURCES - 1)], arr_m.at[slab])

        pack = evolve(slab, arr_s, old_s, hb_s, vb_s, x_s, tend_s, sx)

        def back(n, k):
            row, col = slab * 2 + (a + n) % 2, (b + k) % NY
            return push(tend_s.at[row * NY + col], ret_s.at[me], back_m, ret_m, (row, col))

        for n in range(2):
            for k in range(NY):
                if n or k:
                    back(n, k).start()
        pack()
        pl.when(g < SLABS - 1)(lambda: back(0, 0).start())
        return carry

    lax.fori_loop(0, SLABS, group, 0)
    ret_s[pl.ds(me, 1)] = tend_s[pl.ds(me, 1)]
    settle(send_s.at[pl.ds(0, COLS - 1)], send_m)
    row, col = iota((256, 256), 0), iota((256, 256), 1)
    level = level_of(row)
    grid = jnp.where(col >= LEV, col - LEV, col)
    lift = jnp.where(
        (row // 128 == jnp.where(col >= LEV, 1, 0)) & (level < CLEV) & (col < WIDTH),
        hat(grid, level, (CLEV - 1) / (LEV - 1)),
        0.0,
    ).astype(BF)
    lane = iota((COLS, 256), 1) // 64 % 2
    m0, m1 = onehots(own_ref[...], lambda o: o)
    settle(ret_s.at[pl.ds(0, COLS - 1)], ret_m)
    got = ret_s[:, 0, :].astype(BF)
    got = jnp.where(lane == 0, dot(m0, got, 0, 0), dot(m1, got, 0, 0)).astype(BF)
    gain = dot(got, lift)
    u_s[...] = gain.reshape(NX, NY, 256)
    u_s[:, :, 0:WIDTH] = (gain[:, 0:WIDTH] + gcm_ref[...]).reshape(NX, NY, WIDTH)
    for s in range(2):
        edge_s[s] = u_s[:, 15 * s, :]
    ends = [
        (u_s.at[NX - 1], hx_s.at[0], ((a + 1) % NX, b)),
        (u_s.at[0], hx_s.at[1], ((a + NX - 1) % NX, b)),
        (edge_s.at[1], hy_s.at[0], (a, (b + 1) % NY)),
        (edge_s.at[0], hy_s.at[1], (a, (b + NY - 1) % NY)),
    ]
    copies = [push(src, dst, hs_m.at[i], hr_m.at[i], to) for i, (src, dst, to) in enumerate(ends)]
    for c in copies:
        c.start()
    u = u_s[...].reshape(COLS, 256)
    l_s[...] = pltpu.roll(u, 1, 0).reshape(NX, NY, 256)
    r_s[...] = pltpu.roll(u, COLS - 1, 0).reshape(NX, NY, 256)
    settle(tend_s.at[pl.ds(0, COLS - 1)], back_m)
    for c in copies:
        c.wait()
    l_s[:, 0, :] = hy_s[0]
    r_s[:, NY - 1, :] = hy_s[1]
    up = jnp.concatenate([hx_s[0], u[0:112]], axis=0)
    down = jnp.concatenate([u[16:128], hx_s[1]], axis=0)
    total = up + down + (l_s[...] + r_s[...]).reshape(COLS, 256) - 4.0 * u
    out_ref[...] = u[:, 0:WIDTH] + diff_ref[...] * total[:, 0:WIDTH]


def local(gcm_state, crm_state, owners, ice_mask, horizontal_operator, vertical_inverse, diffusivity):
    vmem, dma = pltpu.VMEM, pltpu.SemaphoreType.DMA
    x = crm_state.reshape(256, 2, 3712).transpose(0, 2, 1).reshape(7424, 128, 2).transpose(0, 2, 1).reshape(14848, 128)
    whole = pl.BlockSpec(memory_space=pltpu.VMEM)
    hbm = pl.BlockSpec(memory_space=pltpu.HBM)
    gcm_out, new = pl.pallas_call(
        step_kernel,
        in_specs=[hbm] * 7,
        out_specs=[whole, whole],
        out_shape=(vmem((COLS, WIDTH), F32), vmem((SLABS, GROUP * ROWS, 128), BF)),
        scratch_shapes=[
            vmem((COLS, WIDTH), F32), vmem((1, COLS), jnp.int32), vmem((COLS, CLEV), jnp.int32),
            vmem((2, CX, CX), BF), vmem((CLEV, 2, CLEV), BF), vmem((1, WIDTH), F32),
            vmem((SLABS, GROUP, 2, 128, 256), BF),
            vmem((GROUP, ROWS + 8, 128), F32),
            vmem((2, 256, 256), BF),
            vmem((256, 256), BF),
            vmem((COLS, 1, 384), F32),
            vmem((COLS, 1, 384), F32),
            vmem((COLS, 1, 256), F32),
            vmem((COLS, 1, 256), F32),
            vmem((NX, NY, 256), F32),
            vmem((NX, NY, 256), F32),
            vmem((NX, NY, 256), F32),
            vmem((2, NY, 256), F32),
            vmem((2, NX, 256), F32),
            vmem((2, NX, 256), F32),
            pltpu.SemaphoreType.REGULAR, dma((6,)), dma((SLABS,)), dma, dma((SLABS,)), dma, dma, dma((4,)), dma((4,)),
        ],
        compiler_params=pltpu.CompilerParams(collective_id=0, has_side_effects=True, vmem_limit_bytes=VMEM_MIB * 2**20),
        name="physics_step",
    )(
        gcm_state.reshape(COLS, WIDTH), owners.reshape(1, COLS), ice_mask.reshape(COLS, CLEV),
        horizontal_operator, vertical_inverse.transpose(1, 0, 2), diffusivity.reshape(1, WIDTH), x,
    )
    new = new.reshape(7424, 2, 128).transpose(0, 2, 1).reshape(256, 3712, 2).transpose(0, 2, 1)
    return gcm_out.reshape(gcm_state.shape), new.reshape(crm_state.shape)


def solution(mesh):
    in_specs = (
        P("gx", "gy", None),
        P(("gx", "gy"), None, None, None, None),
        P(("gx", "gy"), None, None),
        P("gx", "gy", None),
        P(),
        P(),
        P(),
    )
    out_specs = (P("gx", "gy", None), P(("gx", "gy"), None, None, None, None))
    return jax.shard_map(local, mesh=mesh, in_specs=in_specs, out_specs=out_specs, check_vma=False)
```
